128 devices in a mesh: node: 32 (over z, y, core), rep: 4 (over x).
Axes of the slice: x: 4, y: 4, z: 4, core: 2. Of those that a mesh axis runs over, the one named last changes fastest.
Arguments:
- memory: bfloat16 [131072, 256], P('node'), may hold values from -6 to 6
- req_rows: int32 [128, 32, 256], P(('node', 'rep')), may hold values from 0 to 4095, as said below
- src_slot: int32 [131072], P(('node', 'rep')), may hold values from 0 to 7967, as said below
- dst_slot: int32 [131072], P(('node', 'rep')), may hold values from 0 to 8191
- nbr_slot: int32 [131072, 10], P(('node', 'rep')), may hold values from 0 to 8191
- event_time: int32 [131072], P(('node', 'rep')), may hold values from 2000 to 2999
- nbr_time: int32 [131072, 10], P(('node', 'rep')), may hold values from 1000 to 2998, as said below
- frequency: float32 [128], replicated, may hold values from 0.001 to 0.1
- emb_grad: bfloat16 [131072, 256], P(('node', 'rep')), may hold values from -0.03125 to 0.03125
- w_input: bfloat16 [256, 768], replicated, may hold values from -0.375 to 0.375
- w_hidden: bfloat16 [256, 768], replicated, may hold values from -0.375 to 0.375
- w_time: bfloat16 [128, 256], replicated, may hold values from -0.5 to 0.5
- w_query: bfloat16 [256, 256], replicated, may hold values from -0.375 to 0.375
- w_key: bfloat16 [256, 256], replicated, may hold values from -0.375 to 0.375
- w_value: bfloat16 [256, 256], replicated, may hold values from -0.375 to 0.375
- w_out: bfloat16 [256, 256], replicated, may hold values from -0.375 to 0.375
Outputs:
- new_memory: bfloat16 [131072, 256], P('node')
- grad_input: float32 [256, 768], replicated
- grad_hidden: float32 [256, 768], replicated
- grad_time: float32 [128, 256], replicated
- grad_query: float32 [256, 256], replicated
- grad_key: float32 [256, 256], replicated
- grad_value: float32 [256, 256], replicated
- grad_out: float32 [256, 256], replicated
The draws below stay inside these ranges and needn't reach their ends.
Inputs may be any that keep to these rules, and one draw needn't show every extreme that they name: `req_rows`: for each device and owner, 256 distinct rows of that owner's 4096 rows. `src_slot`: the position s % 256 is below 32, so a device's updated rows lie in the leading 32 slots of each owner's list. `nbr_time`: each lies 1 to 1000 below its event's time.
All inputs are finite; a program needn't handle non-finite values.
Results may differ from the reference program's by a relative error of at most 0.014.
Values may be sent and summed in bfloat16 or wider, within the bound.
No kernel may reach another device: no remote copies, remote signals or barrier semaphores. Data moves between devices by JAX's collectives and lax.ppermute only.
A program may use at most 128 MiB of HBM per device.

```python
import math
import jax
import jax.numpy as jnp
from jax import lax

D = 256
HEADS = 8
TD = 128
NBRS = 10
CAP = 256
UCAP = 32
NODE_DEV = 4096
E_DEV = 1024
NODES = 131072
EVENTS = 131072
N_NODE = 32
N_REP = 4


def slot_limits(seed_key):
    devices = N_NODE * N_REP
    base_key = jax.random.fold_in(seed_key, 71)
    full_owner = jax.random.randint(jax.random.fold_in(base_key, 1), (devices, 1), 0, N_NODE)
    device_ids = jnp.arange(devices, dtype=jnp.int32)[:, None]
    full_owner = jnp.where(device_ids == 0, N_NODE - 1, full_owner)
    owner_ids = jnp.arange(N_NODE, dtype=jnp.int32)[None, :]
    read_count = jax.random.randint(jax.random.fold_in(base_key, 2), (devices, N_NODE), CAP // 4, CAP + 1)
    write_count = jax.random.randint(jax.random.fold_in(base_key, 3), (devices, N_NODE), max(1, UCAP // 4), UCAP + 1)
    read_count = jnp.where(owner_ids == full_owner, CAP, read_count)
    write_count = jnp.where(owner_ids == full_owner, UCAP, write_count)
    return (read_count, write_count)


def pick_slots(limits, seed_key, row_width):
    devices = limits.shape[0]
    owner_pick = jax.random.randint(jax.random.fold_in(seed_key, 1), (devices, E_DEV * row_width), 0, N_NODE)
    slot_bound = jnp.take_along_axis(limits, owner_pick, axis=1)
    within = jax.random.randint(jax.random.fold_in(seed_key, 2), owner_pick.shape, 0, slot_bound)
    flat = owner_pick * CAP + within
    flat = flat.at[0, 0].set((N_NODE - 1) * CAP + limits[0, N_NODE - 1] - 1)
    flat = flat.at[0, 1].set(0)
    return flat.reshape(devices * E_DEV, row_width).astype(jnp.int32)


def time_pair(seed_key):
    total = E_DEV * N_NODE * N_REP
    time_key = jax.random.fold_in(seed_key, 53)
    event_times = 2000 + jax.random.randint(jax.random.fold_in(time_key, 1), (total,), 0, 1000)
    spacing = jax.random.randint(jax.random.fold_in(time_key, 2), (total, NBRS), 1, 1001)
    event_times = event_times.at[0].set(2000).at[1].set(2999)
    spacing = spacing.at[0, 0].set(1000).at[1, 0].set(1)
    return (event_times.astype(jnp.int32), (event_times[:, None] - spacing).astype(jnp.int32))


def draw_req_rows(key, part):
    key = jax.random.fold_in(key, 11)
    split_keys = jax.random.split(key, N_NODE * N_REP * N_NODE)
    chosen = jax.vmap(lambda one_key: jax.random.permutation(one_key, NODE_DEV)[:CAP])(split_keys)
    return chosen.reshape(N_NODE * N_REP, N_NODE, CAP).astype(jnp.int32)


def draw_src_slot(key, part):
    read_count, write_count = slot_limits(key)
    key = jax.random.fold_in(key, 3)
    return pick_slots(write_count, key, 1).reshape(-1)


def draw_dst_slot(key, part):
    read_count, write_count = slot_limits(key)
    key = jax.random.fold_in(key, 5)
    return pick_slots(read_count, key, 1).reshape(-1)


def draw_nbr_slot(key, part):
    read_count, write_count = slot_limits(key)
    key = jax.random.fold_in(key, 7)
    return pick_slots(read_count, key, NBRS)


def draw_event_time(key, part):
    event_times, neighbour_times = time_pair(key)
    return event_times


def draw_nbr_time(key, part):
    event_times, neighbour_times = time_pair(key)
    return neighbour_times


def levels(key, dims, cuts, low, high):
    factor_of, own = 1.0, jax.random.fold_in(key, 6)
    for position, parts in cuts:
        heights = jnp.exp(jax.random.uniform(jax.random.fold_in(own, position), (parts,), jnp.float32, low / len(cuts), high / len(cuts)))
        factor_of = factor_of * jnp.repeat(heights, dims[position] // parts).reshape([-1 if axis == position else 1 for axis in range(len(dims))])
    return factor_of


def centred(own_key, dims, width, reach, cuts=(), kind=jnp.bfloat16):
    result = jax.random.normal(own_key, dims, jnp.float32) * width
    if len(cuts) > 0:
        result = levels(own_key, dims, cuts, -0.22, 0.18) * result
    return jnp.clip(result, min=-reach, max=reach).astype(kind)


def setup_inputs(seed: int = 0) -> dict:
    key_of = jax.random.split(jax.random.key(seed), 17)
    memory = centred(key_of[0], (NODES, D), 1.0, 6.0, ((0, 32),))
    req_rows = draw_req_rows(jax.random.fold_in(key_of[16], 71), 0)
    src_slot = draw_src_slot(jax.random.fold_in(key_of[16], 71), 0)
    dst_slot = draw_dst_slot(jax.random.fold_in(key_of[16], 71), 0)
    nbr_slot = draw_nbr_slot(jax.random.fold_in(key_of[16], 71), 0)
    event_time = draw_event_time(jax.random.fold_in(key_of[16], 71), 0)
    nbr_time = draw_nbr_time(jax.random.fold_in(key_of[16], 71), 0)
    frequency = jnp.clip(jnp.exp(jax.random.uniform(key_of[7], (TD,), jnp.float32, math.log(0.001), math.log(0.1))), 0.001, 0.1)
    emb_grad = centred(key_of[8], (EVENTS, D), (2.0 / (E_DEV * N_NODE * N_REP) ** 0.5), 0.03125, ((0, 128),))
    w_input = centred(key_of[9], (D, 3 * D), D ** -0.5, 0.375)
    w_hidden = centred(key_of[10], (D, 3 * D), D ** -0.5, 0.375)
    w_time = centred(key_of[11], (TD, D), TD ** -0.5, 0.5)
    w_query = centred(key_of[12], (D, D), D ** -0.5, 0.375)
    w_key = centred(key_of[13], (D, D), D ** -0.5, 0.375)
    w_value = centred(key_of[14], (D, D), D ** -0.5, 0.375)
    w_out = centred(key_of[15], (D, D), D ** -0.5, 0.375)
    return dict(memory=memory, req_rows=req_rows, src_slot=src_slot, dst_slot=dst_slot, nbr_slot=nbr_slot, event_time=event_time, nbr_time=nbr_time, frequency=frequency, emb_grad=emb_grad, w_input=w_input, w_hidden=w_hidden, w_time=w_time, w_query=w_query, w_key=w_key, w_value=w_value, w_out=w_out)


def event_forward(weights, frequency, mem_src, mem_dst, mem_nbr, spacing, nudges):
    w_input, w_hidden, w_time, w_query, w_key, w_value, w_out = weights
    row_count, row_width = mem_src.shape
    neighbours = mem_nbr.shape[1]
    head_size = row_width // HEADS
    gate_in = jnp.dot(mem_dst, w_input, preferred_element_type=jnp.float32) + nudges[0]
    gate_hid = jnp.dot(mem_src, w_hidden, preferred_element_type=jnp.float32) + nudges[1]
    reset_gate = jax.nn.sigmoid(gate_in[:, :row_width] + gate_hid[:, :row_width])
    update = jax.nn.sigmoid(gate_in[:, row_width:2 * row_width] + gate_hid[:, row_width:2 * row_width])
    candidate = jnp.tanh(gate_in[:, 2 * row_width:] + reset_gate * gate_hid[:, 2 * row_width:])
    hidden = (1.0 - update) * candidate + update * mem_src.astype(jnp.float32)
    hidden_half = hidden.astype(jnp.bfloat16)
    query = (jnp.dot(hidden_half, w_query, preferred_element_type=jnp.float32) + nudges[2]).astype(jnp.bfloat16)
    phase_rows = jnp.cos(spacing[:, :, None] * frequency).astype(jnp.bfloat16).reshape(row_count * neighbours, -1)
    mixed_rows = mem_nbr.reshape(row_count * neighbours, row_width).astype(jnp.float32)
    mixed_rows = mixed_rows + jnp.dot(phase_rows, w_time, preferred_element_type=jnp.float32) + nudges[3]
    mixed_rows = mixed_rows.astype(jnp.bfloat16)
    key_rows = (jnp.dot(mixed_rows, w_key, preferred_element_type=jnp.float32) + nudges[4]).astype(jnp.bfloat16)
    value_rows = (jnp.dot(mixed_rows, w_value, preferred_element_type=jnp.float32) + nudges[5]).astype(jnp.bfloat16)
    key_rows = key_rows.reshape(row_count, neighbours, HEADS, head_size)
    value_rows = value_rows.reshape(row_count, neighbours, HEADS, head_size)
    query_heads = query.reshape(row_count, HEADS, head_size)
    scores = jnp.einsum('ehd,ekhd->ehk', query_heads.astype(jnp.float32), key_rows.astype(jnp.float32)) * head_size ** (-0.5)
    exponent = jnp.exp(scores)
    attention = (exponent / lax.optimization_barrier(jnp.sum(exponent, axis=2, keepdims=True))).astype(jnp.bfloat16)
    attended = jnp.einsum('ehk,ekhd->ehd', attention.astype(jnp.float32), value_rows.astype(jnp.float32))
    attended = attended.astype(jnp.bfloat16).reshape(row_count, row_width)
    embedding = jnp.dot(attended, w_out, preferred_element_type=jnp.float32) + nudges[6] + hidden
    return (embedding, (hidden, hidden_half, phase_rows, mixed_rows, attended))

def outer_sum(left_rows, slope):
    return lax.dot_general(left_rows, slope.astype(jnp.bfloat16), (((0,), (0,)), ((), ())), preferred_element_type=jnp.float32)

def event_grads(weights, frequency, mem_src, mem_dst, mem_nbr, spacing, slope_in):
    row_count, row_width = mem_src.shape
    flat_rows = row_count * mem_nbr.shape[1]
    nudges = (jnp.zeros((row_count, 3 * row_width), jnp.float32), jnp.zeros((row_count, 3 * row_width), jnp.float32), jnp.zeros((row_count, row_width), jnp.float32), jnp.zeros((flat_rows, row_width), jnp.float32), jnp.zeros((flat_rows, row_width), jnp.float32), jnp.zeros((flat_rows, row_width), jnp.float32), jnp.zeros((row_count, row_width), jnp.float32))

    def forward(shifts):
        return event_forward(weights, frequency, mem_src, mem_dst, mem_nbr, spacing, shifts)
    embedding, pullback, saved_terms = jax.vjp(forward, nudges, has_aux=True)
    slopes = pullback(slope_in.astype(jnp.float32))[0]
    hidden, hidden_half, phase_rows, mixed_rows, attended = saved_terms
    weight_grads = (outer_sum(mem_dst, slopes[0]), outer_sum(mem_src, slopes[1]), outer_sum(phase_rows, slopes[3]), outer_sum(hidden_half, slopes[2]), outer_sum(mixed_rows, slopes[4]), outer_sum(mixed_rows, slopes[5]), outer_sum(attended, slopes[6]))
    return (weight_grads, hidden)

def reference(memory, req_rows, src_slot, dst_slot, nbr_slot, event_time, nbr_time, frequency, emb_grad, w_input, w_hidden, w_time, w_query, w_key, w_value, w_out):
    weights = (w_input, w_hidden, w_time, w_query, w_key, w_value, w_out)
    devices = N_NODE * N_REP
    row_width = memory.shape[1]
    base_rows = (jnp.arange(N_NODE, dtype=jnp.int32) * NODE_DEV)[None, :, None]
    global_rows = (req_rows + base_rows).reshape(devices, N_NODE * CAP).astype(jnp.int32)
    spacing_all = (event_time[:, None] - nbr_time).astype(jnp.float32)
    blocks = (global_rows, src_slot.reshape(devices, E_DEV), dst_slot.reshape(devices, E_DEV), nbr_slot.reshape(devices, E_DEV, NBRS), spacing_all.reshape(devices, E_DEV, NBRS), emb_grad.reshape(devices, E_DEV, row_width))

    def one_device(state_pair, block_data):
        totals, change = state_pair
        row_table, source, target, neighbour, spacing, slope_in = block_data
        source_rows = row_table[source]
        mem_src = memory[source_rows]
        mem_dst = memory[row_table[target]]
        mem_nbr = memory[row_table[neighbour]]
        weight_grads, hidden = event_grads(weights, frequency, mem_src, mem_dst, mem_nbr, spacing, slope_in)
        totals = jax.tree.map(jnp.add, totals, weight_grads)
        change = change.at[source_rows].add(hidden - mem_src.astype(jnp.float32))
        return ((totals, change), None)
    start = (jax.tree.map(lambda weight: jnp.zeros(weight.shape, jnp.float32), weights), jnp.zeros(memory.shape, jnp.float32))
    (totals, change), _ = lax.scan(one_device, start, blocks)
    new_memory = (memory.astype(jnp.float32) + change).astype(jnp.bfloat16)
    return (new_memory, totals[0], totals[1], totals[2], totals[3], totals[4], totals[5], totals[6])
```

```python
import math

import jax
import jax.numpy as jnp
from jax import lax
from jax.experimental import pallas as pl
from jax.experimental.pallas import tpu as pltpu
from jax.sharding import PartitionSpec as P

HEADS = 8
UCAP = 32
F32 = jnp.float32
BF16 = jnp.bfloat16
VMEM = pl.BlockSpec(memory_space=pltpu.VMEM)
SMEM = pl.BlockSpec(memory_space=pltpu.SMEM)
LIMIT = 58 * 1024 * 1024


def dot(a, b):
    return jnp.dot(a, b, preferred_element_type=F32)


def dot_nt(a, b):
    return lax.dot_general(a, b, (((1,), (1,)), ((), ())), preferred_element_type=F32)


def dot_tn(a, b):
    return lax.dot_general(a, b, (((0,), (0,)), ((), ())), preferred_element_type=F32)


def spread_table(rows_ref, table, base, step):
    count = rows_ref.shape[0]

    def body(i, carry):
        block = rows_ref[pl.ds(pl.multiple_of(i * step, step), step), :].astype(F32)
        start = base + i * (2 * step)
        table[pl.ds(start, step, stride=2), :] = block[:, :128]
        table[pl.ds(start + 1, step, stride=2), :] = block[:, 128:]
        return carry

    lax.fori_loop(0, count // step, body, 0)


def pick_rows(index_ref, offset, table, stage, count):
    for r in range(count):
        row = index_ref[offset + r]
        stage[2 * r : 2 * r + 2, :] = table[pl.ds(2 * row, 2), :]


def joined(stage, start, count):
    left = stage[pl.ds(2 * start, count, stride=2), :]
    right = stage[pl.ds(2 * start + 1, count, stride=2), :]
    return jnp.concatenate([left, right], axis=1)


def serve_kernel(index_ref, rows_ref, out_ref, table, stage):
    spread_table(rows_ref, table, 0, 256)
    step = stage.shape[0] // 2

    def body(i, carry):
        base = pl.multiple_of(i * step, step)
        pick_rows(index_ref, base, table, stage, step)
        out_ref[pl.ds(base, step), :] = joined(stage, 0, step).astype(BF16)
        return carry

    lax.fori_loop(0, out_ref.shape[0] // step, body, 0)


def serve(index, memory):
    count = index.shape[0]
    rows, width = memory.shape
    return pl.pallas_call(
        serve_kernel,
        out_shape=jax.ShapeDtypeStruct((count, width), BF16),
        in_specs=[SMEM, VMEM],
        out_specs=VMEM,
        scratch_shapes=[pltpu.VMEM((2 * rows, 128), F32), pltpu.VMEM((256, 128), F32)],
        compiler_params=pltpu.CompilerParams(vmem_limit_bytes=LIMIT),
        name="serve_rows",
    )(index, memory)


def sigmoid(x):
    return 1.0 / (1.0 + jnp.exp(-x))


def gru_forward(mem_src, mem_dst, w_input_ref, w_hidden_ref):
    width = mem_src.shape[1]
    parts_in = [dot(mem_dst, w_input_ref[:, k * width : (k + 1) * width]) for k in range(3)]
    parts_hid = [dot(mem_src, w_hidden_ref[:, k * width : (k + 1) * width]) for k in range(3)]
    reset = sigmoid(parts_in[0] + parts_hid[0])
    update = sigmoid(parts_in[1] + parts_hid[1])
    candidate = jnp.tanh(parts_in[2] + reset * parts_hid[2])
    rows = mem_src.astype(F32)
    hidden = (1.0 - update) * candidate + update * rows
    return rows, reset, update, candidate, parts_hid[2], hidden


def memory_kernel(
    src_ref, dst_ref, src_row_ref, rows_ref, w_input_ref, w_hidden_ref,
    mem_src_ref, mem_dst_ref, change_ref, table, stage, delta,
):
    spread_table(rows_ref, table, 0, 256)
    step = stage.shape[0] // 4
    events = mem_src_ref.shape[0]

    def body(i, carry):
        base = pl.multiple_of(i * step, step)
        pick_rows(src_ref, base, table, stage, step)
        pick_rows(dst_ref, base, table, stage.at[pl.ds(2 * step, 2 * step)], step)
        mem_src = joined(stage, 0, step).astype(BF16)
        mem_dst = joined(stage, step, step).astype(BF16)
        mem_src_ref[pl.ds(base, step), :] = mem_src
        mem_dst_ref[pl.ds(base, step), :] = mem_dst
        rows, _, _, _, _, hidden = gru_forward(mem_src, mem_dst, w_input_ref, w_hidden_ref)
        delta[pl.ds(base, step), :] = (hidden - rows).astype(BF16)
        return carry

    lax.fori_loop(0, events // step, body, 0)
    source = src_row_ref[...]
    slot = (source >> 8) * UCAP + (source & 255)
    slots = change_ref.shape[0]
    part = 256
    for k in range(slots // part):
        ids = lax.broadcasted_iota(jnp.int32, (part, events), 0) + k * part
        picked = jnp.where(ids == slot, 1.0, 0.0).astype(BF16)
        change_ref[pl.ds(k * part, part), :] = dot(picked, delta[...]).astype(BF16)


def memory_step(src_slot, dst_slot, fetched, w_input, w_hidden):
    events = src_slot.shape[0]
    count, width = fetched.shape
    slots = count // 256 * UCAP
    return pl.pallas_call(
        memory_kernel,
        out_shape=(
            jax.ShapeDtypeStruct((events, width), BF16),
            jax.ShapeDtypeStruct((events, width), BF16),
            jax.ShapeDtypeStruct((slots, width), BF16),
        ),
        in_specs=[SMEM, SMEM, VMEM, VMEM, VMEM, VMEM],
        out_specs=(VMEM, VMEM, VMEM),
        scratch_shapes=[
            pltpu.VMEM((2 * count, 128), F32),
            pltpu.VMEM((512, 128), F32),
            pltpu.VMEM((events, width), BF16),
        ],
        compiler_params=pltpu.CompilerParams(vmem_limit_bytes=LIMIT),
        name="memory_step",
    )(src_slot, dst_slot, src_slot.reshape(1, events), fetched, w_input, w_hidden)


COS_TERMS = (
    1.0,
    -0.49999988079071045,
    0.041666485369205475,
    -0.001388777862302959,
    2.4769342417130247e-05,
    -2.7073761543761066e-07,
    1.7225967319234314e-09,
)
TURN_HIGH = 6.28125
TURN_LOW = 2.0 * math.pi - 6.28125


def cosine(x):
    turns = jnp.floor(x * (0.5 / math.pi) + 0.5)
    rest = (x - turns * TURN_HIGH) - turns * TURN_LOW
    square = rest * rest
    total = jnp.full_like(x, COS_TERMS[-1])
    for term in COS_TERMS[-2::-1]:
        total = total * square + term
    return total


def events_kernel(
    nbr_ref, rows_ref, spacing_ref, freq_ref, mem_src_ref, mem_dst_ref, slope_ref,
    w_input_ref, w_hidden_ref, w_time_ref, w_query_ref, w_key_ref, w_value_ref, w_out_ref,
    grads_ref,
    table, stage, ones, phase, mixed, keys, values, score, dprob, slopes, dmixed,
    acc_in, acc_hid, acc_time, acc_query, acc_kv, acc_out,
):
    nbrs = spacing_ref.shape[0]
    events, width = slope_ref.shape
    size = stage.shape[0] // (2 * nbrs)
    head = width // HEADS
    scale = head ** -0.5
    spread_table(rows_ref, table, 0, 256)
    row_id = lax.broadcasted_iota(jnp.int32, (width, width), 0) // head
    col_id = lax.broadcasted_iota(jnp.int32, (width, width), 1) // head
    ones[...] = jnp.where(row_id == col_id, 1.0, 0.0).astype(BF16)
    for acc in (acc_in, acc_hid, acc_time, acc_query, acc_kv, acc_out):
        acc[...] = jnp.zeros_like(acc)

    def body(b, carry):
        base = pl.multiple_of(b * size, size)

        def pick(i, c):
            first = i * 128
            j = first // size
            offset = j * events + base + (first - j * size)
            pick_rows(nbr_ref, offset, table, stage.at[pl.ds(pl.multiple_of(2 * first, 256), 256)], 128)
            return c

        lax.fori_loop(0, nbrs * size // 128, pick, 0)
        mem_src = mem_src_ref[pl.ds(base, size), :]
        mem_dst = mem_dst_ref[pl.ds(base, size), :]
        rows, reset, update, candidate, hid_c, hidden = gru_forward(
            mem_src, mem_dst, w_input_ref, w_hidden_ref
        )
        hidden_half = hidden.astype(BF16)
        query = dot(hidden_half, w_query_ref[...]).astype(BF16).astype(F32) * scale
        query_two = query * math.log2(math.e)
        for j in range(nbrs):
            span = pl.ds(j * size, size)
            angle = freq_ref[...] * spacing_ref[j : j + 1, pl.ds(base, size)]
            wave = cosine(angle).astype(BF16)
            phase[:, span] = wave
            mixed[span, :] = (joined(stage, j * size, size) + dot_tn(wave, w_time_ref[...])).astype(BF16)
        for j in range(nbrs):
            span = pl.ds(j * size, size)
            key = dot(mixed[span, :], w_key_ref[...])
            keys[span, :] = key.astype(BF16)
            values[span, :] = dot(mixed[span, :], w_value_ref[...]).astype(BF16)
            score[span, :] = dot((key * query_two).astype(BF16), ones[...])
        top = score[0:size, :]
        for j in range(1, nbrs):
            top = jnp.maximum(top, score[j * size : (j + 1) * size, :])
        total = jnp.zeros_like(top)
        for j in range(nbrs):
            span = pl.ds(j * size, size)
            weight = jnp.exp2(score[span, :] - top)
            score[span, :] = weight
            total = total + weight
        inverse = 1.0 / total
        slope = slope_ref[pl.ds(base, size), :]
        dattended = dot_nt(slope, w_out_ref[...]).astype(BF16).astype(F32)
        attended = jnp.zeros_like(top)
        overlap = jnp.zeros_like(top)
        for j in range(nbrs):
            span = pl.ds(j * size, size)
            prob = score[span, :] * inverse
            score[span, :] = prob
            prob_half = prob.astype(BF16).astype(F32)
            value = values[span, :].astype(F32)
            attended = attended + prob_half * value
            dvalue = (prob_half * dattended).astype(BF16)
            slopes[span, width:] = dvalue
            change = dot((dattended * value).astype(BF16), ones[...])
            dprob[span, :] = change
            overlap = overlap + prob * change
        attended_half = attended.astype(BF16)
        acc_out[...] += dot_tn(attended_half, slope)
        dquery = jnp.zeros_like(top)
        for j in range(nbrs):
            span = pl.ds(j * size, size)
            dscore = score[span, :] * (dprob[span, :] - overlap)
            dquery = dquery + dscore * keys[span, :].astype(F32)
            slopes[span, :width] = (dscore * query).astype(BF16)
        for j in range(nbrs):
            span = pl.ds(j * size, size)
            dmixed[span, :] = (
                dot_nt(slopes[span, :width], w_key_ref[...]) + dot_nt(slopes[span, width:], w_value_ref[...])
            ).astype(BF16)
        acc_kv[...] += dot_tn(mixed[...], slopes[...])
        acc_time[...] += dot(phase[...], dmixed[...])
        dquery_half = (dquery * scale).astype(BF16)
        acc_query[...] += dot_tn(hidden_half, dquery_half)
        dhidden = slope.astype(F32) + dot_nt(dquery_half, w_query_ref[...])
        dcand = dhidden * (1.0 - update) * (1.0 - candidate * candidate)
        dupdate = dhidden * (rows - candidate) * update * (1.0 - update)
        dreset = dcand * hid_c * reset * (1.0 - reset)
        dreset = dreset.astype(BF16)
        dupdate = dupdate.astype(BF16)
        for k, part in enumerate((dreset, dupdate, dcand.astype(BF16))):
            acc_in[:, k * width : (k + 1) * width] += dot_tn(mem_dst, part)
        for k, part in enumerate((dreset, dupdate, (dcand * reset).astype(BF16))):
            acc_hid[:, k * width : (k + 1) * width] += dot_tn(mem_src, part)
        return carry

    lax.fori_loop(0, events // size, body, 0)
    row = 0
    for acc in (acc_in, acc_hid, acc_time, acc_query, acc_kv, acc_out):
        depth, columns = acc.shape
        for k in range(columns // 128):
            grads_ref[row : row + depth, :] = acc[:, k * 128 : (k + 1) * 128].astype(BF16)
            row += depth
    if row < grads_ref.shape[0]:
        grads_ref[row:, :] = jnp.zeros((grads_ref.shape[0] - row, 128), BF16)


def events_step(nbr_index, fetched, spacing, frequency, mem_src, mem_dst, slope, weights, grad_rows, size=256):
    nbrs, events = spacing.shape
    count, width = fetched.shape
    freqs = frequency.shape[0]
    flat = nbrs * size
    return pl.pallas_call(
        events_kernel,
        out_shape=jax.ShapeDtypeStruct((grad_rows, 128), BF16),
        in_specs=[SMEM] + [VMEM] * 13,
        out_specs=VMEM,
        scratch_shapes=[
            pltpu.VMEM((2 * count, 128), F32),
            pltpu.VMEM((2 * flat, 128), F32),
            pltpu.VMEM((width, width), BF16),
            pltpu.VMEM((freqs, flat), BF16),
            pltpu.VMEM((flat, width), BF16),
            pltpu.VMEM((flat, width), BF16),
            pltpu.VMEM((flat, width), BF16),
            pltpu.VMEM((flat, width), F32),
            pltpu.VMEM((flat, width), F32),
            pltpu.VMEM((flat, 2 * width), BF16),
            pltpu.VMEM((flat, width), BF16),
            pltpu.VMEM((width, 3 * width), F32),
            pltpu.VMEM((width, 3 * width), F32),
            pltpu.VMEM((freqs, width), F32),
            pltpu.VMEM((width, width), F32),
            pltpu.VMEM((width, 2 * width), F32),
            pltpu.VMEM((width, width), F32),
        ],
        compiler_params=pltpu.CompilerParams(vmem_limit_bytes=LIMIT),
        name="events_step",
    )(nbr_index, fetched, spacing, frequency.reshape(freqs, 1), mem_src, mem_dst, slope, *weights)


def merge_kernel(index_ref, change_ref, memory_ref, out_ref, table, stage):
    rows = memory_ref.shape[0]
    spread_table(memory_ref, table, 0, 256)
    step = stage.shape[0] // 2
    group = 32

    def body(i, carry):
        base = pl.multiple_of(i * step, step)
        block = change_ref[pl.ds(base, step), :].astype(F32)
        stage[pl.ds(0, step, stride=2), :] = block[:, :128]
        stage[pl.ds(1, step, stride=2), :] = block[:, 128:]
        for g in range(step // group):
            spots = [pl.ds(2 * index_ref[base + g * group + r], 2) for r in range(group)]
            sums = [
                table[spots[r], :] + stage[2 * (g * group + r) : 2 * (g * group + r) + 2, :]
                for r in range(group)
            ]
            for r in range(group):
                table[spots[r], :] = sums[r]
        return carry

    lax.fori_loop(0, change_ref.shape[0] // step, body, 0)

    def finish(i, carry):
        base = pl.multiple_of(i * 256, 256)
        left = table[pl.ds(2 * base, 256, stride=2), :]
        right = table[pl.ds(2 * base + 1, 256, stride=2), :]
        out_ref[pl.ds(base, 256), :] = jnp.concatenate([left, right], axis=1).astype(BF16)
        return carry

    lax.fori_loop(0, rows // 256, finish, 0)


def merge(index, change, memory):
    rows, width = memory.shape
    return pl.pallas_call(
        merge_kernel,
        out_shape=jax.ShapeDtypeStruct((rows, width), BF16),
        in_specs=[SMEM, VMEM, VMEM],
        out_specs=VMEM,
        scratch_shapes=[pltpu.VMEM((2 * rows, 128), F32), pltpu.VMEM((256, 128), F32)],
        compiler_params=pltpu.CompilerParams(vmem_limit_bytes=LIMIT),
        name="merge_rows",
    )(index, change, memory)


def total_kernel(parts_ref, out_ref):
    total = jnp.zeros(parts_ref.shape[1:], F32)
    for k in range(parts_ref.shape[0]):
        total = total + parts_ref[k].astype(F32)
    total = total.astype(BF16)
    for k in range(parts_ref.shape[0]):
        out_ref[k] = total


def total_parts(parts):
    return pl.pallas_call(
        total_kernel,
        out_shape=jax.ShapeDtypeStruct(parts.shape, BF16),
        in_specs=[VMEM],
        out_specs=VMEM,
        compiler_params=pltpu.CompilerParams(vmem_limit_bytes=LIMIT),
        name="total_parts",
    )(parts)


def unpack_kernel(flat_ref, *out_refs):
    row = 0
    for out_ref in out_refs:
        depth, columns = out_ref.shape
        for k in range(columns // 128):
            out_ref[:, k * 128 : (k + 1) * 128] = flat_ref[row : row + depth, :].astype(F32)
            row += depth


def unpack(flat, shapes):
    return pl.pallas_call(
        unpack_kernel,
        out_shape=tuple(jax.ShapeDtypeStruct(shape, F32) for shape in shapes),
        in_specs=[VMEM],
        out_specs=tuple(VMEM for _ in shapes),
        compiler_params=pltpu.CompilerParams(vmem_limit_bytes=LIMIT),
        name="unpack_grads",
    )(flat)


BOTH = ("node", "rep")


def local(
    memory, req_rows, src_slot, dst_slot, nbr_slot, event_time, nbr_time, frequency, emb_grad,
    w_input, w_hidden, w_time, w_query, w_key, w_value, w_out,
):
    weights = (w_input, w_hidden, w_time, w_query, w_key, w_value, w_out)
    requests = req_rows[0]
    owners, capacity = requests.shape
    width = memory.shape[1]
    reps = lax.axis_size("rep")
    asked = lax.all_to_all(requests, "node", split_axis=0, concat_axis=0, tiled=True)
    served = serve(asked.reshape(-1), memory).reshape(owners, capacity, width)
    fetched = lax.all_to_all(served, "node", split_axis=0, concat_axis=0, tiled=True)
    fetched = fetched.reshape(owners * capacity, width)
    nbr_index = nbr_slot.T.reshape(-1)
    spacing = (event_time[None, :] - nbr_time.T).astype(F32)
    mem_src, mem_dst, change = memory_step(src_slot, dst_slot, fetched, w_input, w_hidden)
    spread = jnp.broadcast_to(
        change.reshape(owners, 1, UCAP, width), (owners, reps, UCAP, width)
    ).reshape(owners * reps * UCAP, width)
    updates = lax.all_to_all(spread, BOTH, split_axis=0, concat_axis=0, tiled=True)
    touched = lax.all_gather(asked[:, :UCAP], "rep")
    touched = jnp.transpose(touched, (1, 0, 2)).reshape(-1)
    shapes = (w_input.shape, w_hidden.shape, w_time.shape, w_query.shape, w_key.shape, w_value.shape, w_out.shape)
    used = sum(shape[0] * shape[1] for shape in shapes) // 128
    devices = owners * reps
    share = -(-used // (devices * 16)) * 16
    grads = events_step(nbr_index, fetched, spacing, frequency, mem_src, mem_dst, emb_grad, weights, devices * share)
    parts = lax.all_to_all(grads, BOTH, split_axis=0, concat_axis=0, tiled=True)
    summed = total_parts(parts.reshape(devices, share, 128))
    flat = lax.all_to_all(summed.reshape(devices * share, 128), BOTH, split_axis=0, concat_axis=0, tiled=True)
    new_memory = merge(touched, updates, memory)
    return (new_memory, *unpack(flat, shapes))


def solution(mesh):
    split = P(BOTH)
    placed = (
        P("node", None), P(BOTH, None, None), split, split, P(BOTH, None), split, P(BOTH, None),
        P(), P(BOTH, None), P(), P(), P(), P(), P(), P(), P(),
    )
    return jax.shard_map(
        local,
        mesh=mesh,
        in_specs=placed,
        out_specs=(P("node", None), P(), P(), P(), P(), P(), P(), P()),
        check_vma=False,
    )
```

```python
import math

import jax
import jax.numpy as jnp
from jax import lax
from jax.experimental import pallas as pl
from jax.experimental.pallas import tpu as pltpu
from jax.sharding import PartitionSpec as P

HEADS = 8
UCAP = 32
F32 = jnp.float32
BF16 = jnp.bfloat16
VMEM = pl.BlockSpec(memory_space=pltpu.VMEM)
SMEM = pl.BlockSpec(memory_space=pltpu.SMEM)
LIMIT = 58 * 1024 * 1024


def cost(micros):
    return pl.CostEstimate(flops=int(micros * 1.1e9), bytes_accessed=int(micros * 3.0e6), transcendentals=0)


def dot(a, b):
    return jnp.dot(a, b, preferred_element_type=F32)


def dot_nt(a, b):
    return lax.dot_general(a, b, (((1,), (1,)), ((), ())), preferred_element_type=F32)


def dot_tn(a, b):
    return lax.dot_general(a, b, (((0,), (0,)), ((), ())), preferred_element_type=F32)


def spread_table(rows_ref, table, base, step):
    count = rows_ref.shape[0]

    def body(i, carry):
        block = rows_ref[pl.ds(pl.multiple_of(i * step, step), step), :].astype(F32)
        start = base + i * (2 * step)
        table[pl.ds(start, step, stride=2), :] = block[:, :128]
        table[pl.ds(start + 1, step, stride=2), :] = block[:, 128:]
        return carry

    lax.fori_loop(0, count // step, body, 0)


def pick_rows(index_ref, offset, table, stage, count):
    for r in range(count):
        row = index_ref[offset + r]
        stage[2 * r : 2 * r + 2, :] = table[pl.ds(2 * row, 2), :]


def joined(stage, start, count):
    left = stage[pl.ds(2 * start, count, stride=2), :]
    right = stage[pl.ds(2 * start + 1, count, stride=2), :]
    return jnp.concatenate([left, right], axis=1)


def serve_kernel(index_ref, rows_ref, out_ref, table, stage):
    spread_table(rows_ref, table, 0, 256)
    step = stage.shape[0] // 2

    def body(i, carry):
        base = pl.multiple_of(i * step, step)
        pick_rows(index_ref, base, table, stage, step)
        out_ref[pl.ds(base, step), :] = joined(stage, 0, step).astype(BF16)
        return carry

    lax.fori_loop(0, out_ref.shape[0] // step, body, 0)


def serve(index, memory):
    count = index.shape[0]
    rows, width = memory.shape
    return pl.pallas_call(
        serve_kernel,
        out_shape=jax.ShapeDtypeStruct((count, width), BF16),
        in_specs=[SMEM, VMEM],
        out_specs=VMEM,
        scratch_shapes=[pltpu.VMEM((2 * rows, 128), F32), pltpu.VMEM((256, 128), F32)],
        compiler_params=pltpu.CompilerParams(vmem_limit_bytes=LIMIT),
        cost_estimate=cost(13),
        name="serve_rows",
    )(index, memory)


def sigmoid(x):
    return 1.0 / (1.0 + jnp.exp(-x))


def gru_forward(mem_src, mem_dst, w_input_ref, w_hidden_ref):
    width = mem_src.shape[1]
    parts_in = [dot(mem_dst, w_input_ref[:, k * width : (k + 1) * width]) for k in range(3)]
    parts_hid = [dot(mem_src, w_hidden_ref[:, k * width : (k + 1) * width]) for k in range(3)]
    reset = sigmoid(parts_in[0] + parts_hid[0])
    update = sigmoid(parts_in[1] + parts_hid[1])
    candidate = jnp.tanh(parts_in[2] + reset * parts_hid[2])
    rows = mem_src.astype(F32)
    hidden = (1.0 - update) * candidate + update * rows
    return rows, reset, update, candidate, parts_hid[2], hidden


def memory_kernel(
    src_ref, dst_ref, src_row_ref, rows_ref, w_input_ref, w_hidden_ref,
    mem_src_ref, mem_dst_ref, change_ref, table, stage, delta,
):
    spread_table(rows_ref, table, 0, 256)
    step = stage.shape[0] // 4
    events = mem_src_ref.shape[0]

    def body(i, carry):
        base = pl.multiple_of(i * step, step)
        pick_rows(src_ref, base, table, stage, step)
        pick_rows(dst_ref, base, table, stage.at[pl.ds(2 * step, 2 * step)], step)
        mem_src = joined(stage, 0, step).astype(BF16)
        mem_dst = joined(stage, step, step).astype(BF16)
        mem_src_ref[pl.ds(base, step), :] = mem_src
        mem_dst_ref[pl.ds(base, step), :] = mem_dst
        rows, _, _, _, _, hidden = gru_forward(mem_src, mem_dst, w_input_ref, w_hidden_ref)
        delta[pl.ds(base, step), :] = (hidden - rows).astype(BF16)
        return carry

    lax.fori_loop(0, events // step, body, 0)
    source = src_row_ref[...]
    slot = (source >> 8) * UCAP + (source & 255)
    slots = change_ref.shape[0]
    part = 256
    for k in range(slots // part):
        ids = lax.broadcasted_iota(jnp.int32, (part, events), 0) + k * part
        picked = jnp.where(ids == slot, 1.0, 0.0).astype(BF16)
        change_ref[pl.ds(k * part, part), :] = dot(picked, delta[...]).astype(BF16)


def memory_step(src_slot, dst_slot, fetched, w_input, w_hidden):
    events = src_slot.shape[0]
    count, width = fetched.shape
    slots = count // 256 * UCAP
    return pl.pallas_call(
        memory_kernel,
        out_shape=(
            jax.ShapeDtypeStruct((events, width), BF16),
            jax.ShapeDtypeStruct((events, width), BF16),
            jax.ShapeDtypeStruct((slots, width), BF16),
        ),
        in_specs=[SMEM, SMEM, VMEM, VMEM, VMEM, VMEM],
        out_specs=(VMEM, VMEM, VMEM),
        scratch_shapes=[
            pltpu.VMEM((2 * count, 128), F32),
            pltpu.VMEM((512, 128), F32),
            pltpu.VMEM((events, width), BF16),
        ],
        compiler_params=pltpu.CompilerParams(vmem_limit_bytes=LIMIT),
        cost_estimate=cost(8),
        name="memory_step",
    )(src_slot, dst_slot, src_slot.reshape(1, events), fetched, w_input, w_hidden)


COS_TERMS = (
    1.0,
    -0.49999988079071045,
    0.041666485369205475,
    -0.001388777862302959,
    2.4769342417130247e-05,
    -2.7073761543761066e-07,
    1.7225967319234314e-09,
)
TURN_HIGH = 6.28125
TURN_LOW = 2.0 * math.pi - 6.28125


def cosine(x):
    turns = jnp.floor(x * (0.5 / math.pi) + 0.5)
    rest = (x - turns * TURN_HIGH) - turns * TURN_LOW
    square = rest * rest
    total = jnp.full_like(x, COS_TERMS[-1])
    for term in COS_TERMS[-2::-1]:
        total = total * square + term
    return total


def events_kernel(
    nbr_ref, rows_ref, spacing_ref, freq_ref, mem_src_ref, mem_dst_ref, slope_ref,
    w_input_ref, w_hidden_ref, w_time_ref, w_query_ref, w_key_ref, w_value_ref, w_out_ref,
    grads_ref,
    table, stage, ones, phase, mixed, keys, values, score, dprob, slopes, dmixed,
    acc_in, acc_hid, acc_time, acc_query, acc_kv, acc_out,
):
    nbrs = spacing_ref.shape[0]
    events, width = slope_ref.shape
    size = stage.shape[0] // (2 * nbrs)
    head = width // HEADS
    scale = head ** -0.5
    spread_table(rows_ref, table, 0, 256)
    row_id = lax.broadcasted_iota(jnp.int32, (width, width), 0) // head
    col_id = lax.broadcasted_iota(jnp.int32, (width, width), 1) // head
    ones[...] = jnp.where(row_id == col_id, 1.0, 0.0).astype(BF16)
    for acc in (acc_in, acc_hid, acc_time, acc_query, acc_kv, acc_out):
        acc[...] = jnp.zeros_like(acc)

    def body(b, carry):
        base = pl.multiple_of(b * size, size)

        def pick(i, c):
            first = i * 128
            j = first // size
            offset = j * events + base + (first - j * size)
            pick_rows(nbr_ref, offset, table, stage.at[pl.ds(pl.multiple_of(2 * first, 256), 256)], 128)
            return c

        lax.fori_loop(0, nbrs * size // 128, pick, 0)
        mem_src = mem_src_ref[pl.ds(base, size), :]
        mem_dst = mem_dst_ref[pl.ds(base, size), :]
        rows, reset, update, candidate, hid_c, hidden = gru_forward(
            mem_src, mem_dst, w_input_ref, w_hidden_ref
        )
        hidden_half = hidden.astype(BF16)
        query = dot(hidden_half, w_query_ref[...]).astype(BF16).astype(F32) * scale
        query_two = query * math.log2(math.e)
        for j in range(nbrs):
            span = pl.ds(j * size, size)
            angle = freq_ref[...] * spacing_ref[j : j + 1, pl.ds(base, size)]
            wave = cosine(angle).astype(BF16)
            phase[:, span] = wave
            mixed[span, :] = (joined(stage, j * size, size) + dot_tn(wave, w_time_ref[...])).astype(BF16)
        for j in range(nbrs):
            span = pl.ds(j * size, size)
            key = dot(mixed[span, :], w_key_ref[...])
            keys[span, :] = key.astype(BF16)
            values[span, :] = dot(mixed[span, :], w_value_ref[...]).astype(BF16)
            score[span, :] = dot((key * query_two).astype(BF16), ones[...])
        top = score[0:size, :]
        for j in range(1, nbrs):
            top = jnp.maximum(top, score[j * size : (j + 1) * size, :])
        total = jnp.zeros_like(top)
        for j in range(nbrs):
            span = pl.ds(j * size, size)
            weight = jnp.exp2(score[span, :] - top)
            score[span, :] = weight
            total = total + weight
        inverse = 1.0 / total
        slope = slope_ref[pl.ds(base, size), :]
        dattended = dot_nt(slope, w_out_ref[...]).astype(BF16).astype(F32)
        attended = jnp.zeros_like(top)
        overlap = jnp.zeros_like(top)
        for j in range(nbrs):
            span = pl.ds(j * size, size)
            prob = score[span, :] * inverse
            score[span, :] = prob
            prob_half = prob.astype(BF16).astype(F32)
            value = values[span, :].astype(F32)
            attended = attended + prob_half * value
            dvalue = (prob_half * dattended).astype(BF16)
            slopes[span, width:] = dvalue
            change = dot((dattended * value).astype(BF16), ones[...])
            dprob[span, :] = change
            overlap = overlap + prob * change
        attended_half = attended.astype(BF16)
        acc_out[...] += dot_tn(attended_half, slope)
        dquery = jnp.zeros_like(top)
        for j in range(nbrs):
            span = pl.ds(j * size, size)
            dscore = score[span, :] * (dprob[span, :] - overlap)
            dquery = dquery + dscore * keys[span, :].astype(F32)
            slopes[span, :width] = (dscore * query).astype(BF16)
        for j in range(nbrs):
            span = pl.ds(j * size, size)
            dmixed[span, :] = (
                dot_nt(slopes[span, :width], w_key_ref[...]) + dot_nt(slopes[span, width:], w_value_ref[...])
            ).astype(BF16)
        acc_kv[...] += dot_tn(mixed[...], slopes[...])
        acc_time[...] += dot(phase[...], dmixed[...])
        dquery_half = (dquery * scale).astype(BF16)
        acc_query[...] += dot_tn(hidden_half, dquery_half)
        dhidden = slope.astype(F32) + dot_nt(dquery_half, w_query_ref[...])
        dcand = dhidden * (1.0 - update) * (1.0 - candidate * candidate)
        dupdate = dhidden * (rows - candidate) * update * (1.0 - update)
        dreset = dcand * hid_c * reset * (1.0 - reset)
        dreset = dreset.astype(BF16)
        dupdate = dupdate.astype(BF16)
        for k, part in enumerate((dreset, dupdate, dcand.astype(BF16))):
            acc_in[:, k * width : (k + 1) * width] += dot_tn(mem_dst, part)
        for k, part in enumerate((dreset, dupdate, (dcand * reset).astype(BF16))):
            acc_hid[:, k * width : (k + 1) * width] += dot_tn(mem_src, part)
        return carry

    lax.fori_loop(0, events // size, body, 0)
    row = 0
    for acc in (acc_in, acc_hid, acc_time, acc_query, acc_kv, acc_out):
        depth, columns = acc.shape
        for k in range(columns // 128):
            grads_ref[row : row + depth, :] = acc[:, k * 128 : (k + 1) * 128].astype(BF16)
            row += depth
    if row < grads_ref.shape[0]:
        grads_ref[row:, :] = jnp.zeros((grads_ref.shape[0] - row, 128), BF16)


def events_step(nbr_index, fetched, spacing, frequency, mem_src, mem_dst, slope, weights, grad_rows, size=256):
    nbrs, events = spacing.shape
    count, width = fetched.shape
    freqs = frequency.shape[0]
    flat = nbrs * size
    return pl.pallas_call(
        events_kernel,
        out_shape=jax.ShapeDtypeStruct((grad_rows, 128), BF16),
        in_specs=[SMEM] + [VMEM] * 13,
        out_specs=VMEM,
        scratch_shapes=[
            pltpu.VMEM((2 * count, 128), F32),
            pltpu.VMEM((2 * flat, 128), F32),
            pltpu.VMEM((width, width), BF16),
            pltpu.VMEM((freqs, flat), BF16),
            pltpu.VMEM((flat, width), BF16),
            pltpu.VMEM((flat, width), BF16),
            pltpu.VMEM((flat, width), BF16),
            pltpu.VMEM((flat, width), F32),
            pltpu.VMEM((flat, width), F32),
            pltpu.VMEM((flat, 2 * width), BF16),
            pltpu.VMEM((flat, width), BF16),
            pltpu.VMEM((width, 3 * width), F32),
            pltpu.VMEM((width, 3 * width), F32),
            pltpu.VMEM((freqs, width), F32),
            pltpu.VMEM((width, width), F32),
            pltpu.VMEM((width, 2 * width), F32),
            pltpu.VMEM((width, width), F32),
        ],
        compiler_params=pltpu.CompilerParams(vmem_limit_bytes=LIMIT),
        cost_estimate=cost(44),
        name="events_step",
    )(nbr_index, fetched, spacing, frequency.reshape(freqs, 1), mem_src, mem_dst, slope, *weights)


def merge_kernel(place_ref, index_ref, change_ref, memory_ref, out_ref, table, stage):
    rows = memory_ref.shape[0]
    spread_table(memory_ref, table, 0, 256)
    step = stage.shape[0] // 2
    group = UCAP
    reps = 4
    owner_rows = change_ref.shape[0] // reps
    here = place_ref[0]

    def body(i, carry):
        base = pl.multiple_of(i * step, step)
        block = change_ref[pl.ds(base, step), :].astype(F32)
        stage[pl.ds(0, step, stride=2), :] = block[:, :128]
        stage[pl.ds(1, step, stride=2), :] = block[:, 128:]
        for g in range(step // group):
            sender = i * (step // group) + g
            first = lax.rem(here - lax.rem(sender, reps) + reps, reps) * owner_rows + sender // reps * group
            spots = [pl.ds(2 * index_ref[first + r], 2) for r in range(group)]
            sums = [
                table[spots[r], :] + stage[2 * (g * group + r) : 2 * (g * group + r) + 2, :]
                for r in range(group)
            ]
            for r in range(group):
                table[spots[r], :] = sums[r]
        return carry

    lax.fori_loop(0, change_ref.shape[0] // step, body, 0)

    def finish(i, carry):
        base = pl.multiple_of(i * 256, 256)
        left = table[pl.ds(2 * base, 256, stride=2), :]
        right = table[pl.ds(2 * base + 1, 256, stride=2), :]
        out_ref[pl.ds(base, 256), :] = jnp.concatenate([left, right], axis=1).astype(BF16)
        return carry

    lax.fori_loop(0, rows // 256, finish, 0)


def merge(place, index, change, memory):
    rows, width = memory.shape
    return pl.pallas_call(
        merge_kernel,
        out_shape=jax.ShapeDtypeStruct((rows, width), BF16),
        in_specs=[SMEM, SMEM, VMEM, VMEM],
        out_specs=VMEM,
        scratch_shapes=[pltpu.VMEM((2 * rows, 128), F32), pltpu.VMEM((256, 128), F32)],
        compiler_params=pltpu.CompilerParams(vmem_limit_bytes=LIMIT),
        cost_estimate=cost(11),
        name="merge_rows",
    )(place, index, change, memory)


def total_kernel(parts_ref, out_ref):
    total = jnp.zeros(parts_ref.shape[1:], F32)
    for k in range(parts_ref.shape[0]):
        total = total + parts_ref[k].astype(F32)
    total = total.astype(BF16)
    for k in range(parts_ref.shape[0]):
        out_ref[k] = total


def total_parts(parts):
    return pl.pallas_call(
        total_kernel,
        out_shape=jax.ShapeDtypeStruct(parts.shape, BF16),
        in_specs=[VMEM],
        out_specs=VMEM,
        compiler_params=pltpu.CompilerParams(vmem_limit_bytes=LIMIT),
        cost_estimate=cost(3),
        name="total_parts",
    )(parts)


def unpack_kernel(flat_ref, *out_refs):
    row = 0
    for out_ref in out_refs:
        depth, columns = out_ref.shape
        for k in range(columns // 128):
            out_ref[:, k * 128 : (k + 1) * 128] = flat_ref[row : row + depth, :].astype(F32)
            row += depth


def unpack(flat, shapes):
    return pl.pallas_call(
        unpack_kernel,
        out_shape=tuple(jax.ShapeDtypeStruct(shape, F32) for shape in shapes),
        in_specs=[VMEM],
        out_specs=tuple(VMEM for _ in shapes),
        compiler_params=pltpu.CompilerParams(vmem_limit_bytes=LIMIT),
        cost_estimate=cost(3),
        name="unpack_grads",
    )(flat)


BOTH = ("node", "rep")


def local(
    memory, req_rows, src_slot, dst_slot, nbr_slot, event_time, nbr_time, frequency, emb_grad,
    w_input, w_hidden, w_time, w_query, w_key, w_value, w_out,
):
    weights = (w_input, w_hidden, w_time, w_query, w_key, w_value, w_out)
    requests = req_rows[0]
    owners, capacity = requests.shape
    width = memory.shape[1]
    reps = lax.axis_size("rep")
    asked = lax.all_to_all(requests, "node", split_axis=0, concat_axis=0, tiled=True)
    served = serve(asked.reshape(-1), memory).reshape(owners, capacity, width)
    fetched = lax.all_to_all(served, "node", split_axis=0, concat_axis=0, tiled=True)
    fetched = fetched.reshape(owners * capacity, width)
    lead = asked[:, :UCAP]
    turned = [lead] + [
        lax.ppermute(lead, "rep", [(i, (i + k) % reps) for i in range(reps)]) for k in range(1, reps)
    ]
    touched = jnp.stack(turned).reshape(-1)
    place = lax.axis_index("rep").astype(jnp.int32).reshape(1)
    fetched, touched = lax.optimization_barrier((fetched, touched))
    nbr_index = nbr_slot.T.reshape(-1)
    spacing = (event_time[None, :] - nbr_time.T).astype(F32)
    mem_src, mem_dst, change = memory_step(src_slot, dst_slot, fetched, w_input, w_hidden)
    spread = jnp.broadcast_to(
        change.reshape(owners, 1, UCAP, width), (owners, reps, UCAP, width)
    ).reshape(owners * reps * UCAP, width)
    updates = lax.all_to_all(spread, BOTH, split_axis=0, concat_axis=0, tiled=True)
    shapes = (w_input.shape, w_hidden.shape, w_time.shape, w_query.shape, w_key.shape, w_value.shape, w_out.shape)
    used = sum(shape[0] * shape[1] for shape in shapes) // 128
    devices = owners * reps
    share = -(-used // (devices * 16)) * 16
    grads = events_step(nbr_index, fetched, spacing, frequency, mem_src, mem_dst, emb_grad, weights, devices * share)
    grads, updates = lax.optimization_barrier((grads, updates))
    parts = lax.all_to_all(grads, BOTH, split_axis=0, concat_axis=0, tiled=True)
    summed = total_parts(parts.reshape(devices, share, 128))
    flat = lax.all_to_all(summed.reshape(devices * share, 128), BOTH, split_axis=0, concat_axis=0, tiled=True)
    new_memory = merge(place, touched, updates, memory)
    return (new_memory, *unpack(flat, shapes))


def solution(mesh):
    split = P(BOTH)
    placed = (
        P("node", None), P(BOTH, None, None), split, split, P(BOTH, None), split, P(BOTH, None),
        P(), P(BOTH, None), P(), P(), P(), P(), P(), P(), P(),
    )
    return jax.shard_map(
        local,
        mesh=mesh,
        in_specs=placed,
        out_specs=(P("node", None), P(), P(), P(), P(), P(), P(), P()),
        check_vma=False,
    )
```

```python
import functools
import math

import jax
import jax.numpy as jnp
from jax import lax
from jax.experimental import pallas as pl
from jax.experimental.pallas import tpu as pltpu
from jax.sharding import PartitionSpec as P

HEADS = 8
UCAP = 32
F32 = jnp.float32
BF16 = jnp.bfloat16
VMEM = pl.BlockSpec(memory_space=pltpu.VMEM)
SMEM = pl.BlockSpec(memory_space=pltpu.SMEM)
LIMIT = 58 * 1024 * 1024


def cost(micros):
    return pl.CostEstimate(flops=int(micros * 1.1e9), bytes_accessed=int(micros * 3.0e6), transcendentals=0)


def dot(a, b):
    return jnp.dot(a, b, preferred_element_type=F32)


def dot_nt(a, b):
    return lax.dot_general(a, b, (((1,), (1,)), ((), ())), preferred_element_type=F32)


def dot_tn(a, b):
    return lax.dot_general(a, b, (((0,), (0,)), ((), ())), preferred_element_type=F32)


def spread_table(rows_ref, table, base, step):
    count = rows_ref.shape[0]

    def body(i, carry):
        block = rows_ref[pl.ds(pl.multiple_of(i * step, step), step), :].astype(F32)
        start = base + i * (2 * step)
        table[pl.ds(start, step, stride=2), :] = block[:, :128]
        table[pl.ds(start + 1, step, stride=2), :] = block[:, 128:]
        return carry

    lax.fori_loop(0, count // step, body, 0)


def pick_rows(index_ref, offset, table, stage, count, start=0):
    for r in range(start, start + count):
        spot = index_ref[offset + r]
        stage[2 * r : 2 * r + 2, :] = table[pl.ds(pl.multiple_of(spot, 2), 2), :]


def joined(stage, start, count):
    left = stage[pl.ds(2 * start, count, stride=2), :]
    right = stage[pl.ds(2 * start + 1, count, stride=2), :]
    return jnp.concatenate([left, right], axis=1)


def serve_kernel(index_ref, rows_ref, out_ref, table, stage):
    block = pl.program_id(0)
    step = stage.shape[0] // 2
    count = out_ref.shape[0]

    @pl.when(block == 0)
    def _():
        spread_table(rows_ref, table, 0, 256)

    def body(i, carry):
        base = pl.multiple_of(i * step, step)
        pick_rows(index_ref, block * count + base, table, stage, step)
        out_ref[pl.ds(base, step), :] = joined(stage, 0, step).astype(BF16)
        return carry

    lax.fori_loop(0, count // step, body, 0)


def serve(index, memory):
    count = index.shape[0]
    rows, width = memory.shape
    blocks = 4
    return pl.pallas_call(
        serve_kernel,
        out_shape=jax.ShapeDtypeStruct((count, width), BF16),
        grid=(blocks,),
        in_specs=[SMEM, VMEM],
        out_specs=pl.BlockSpec((count // blocks, width), lambda i: (i, 0)),
        scratch_shapes=[pltpu.VMEM((2 * rows, 128), F32), pltpu.VMEM((256, 128), F32)],
        compiler_params=pltpu.CompilerParams(vmem_limit_bytes=LIMIT),
        cost_estimate=cost(11),
        name="serve_rows",
    )(index, memory)


def sigmoid(x):
    return 1.0 / (1.0 + jnp.exp(-x))


def gru_forward(mem_src, mem_dst, w_input_ref, w_hidden_ref):
    width = mem_src.shape[1]
    parts_in = [dot(mem_dst, w_input_ref[:, k * width : (k + 1) * width]) for k in range(3)]
    parts_hid = [dot(mem_src, w_hidden_ref[:, k * width : (k + 1) * width]) for k in range(3)]
    reset = sigmoid(parts_in[0] + parts_hid[0])
    update = sigmoid(parts_in[1] + parts_hid[1])
    candidate = jnp.tanh(parts_in[2] + reset * parts_hid[2])
    rows = mem_src.astype(F32)
    hidden = (1.0 - update) * candidate + update * rows
    return rows, reset, update, candidate, parts_hid[2], hidden


def memory_kernel(
    src_ref, dst_ref, src_row_ref, rows_ref, w_input_ref, w_hidden_ref,
    mem_src_ref, mem_dst_ref, change_ref, table, stage, delta,
):
    spread_table(rows_ref, table, 0, 256)
    step = stage.shape[0] // 4
    events = mem_src_ref.shape[0]

    def body(i, carry):
        base = pl.multiple_of(i * step, step)
        pick_rows(src_ref, base, table, stage, step)
        pick_rows(dst_ref, base, table, stage.at[pl.ds(2 * step, 2 * step)], step)
        mem_src = joined(stage, 0, step).astype(BF16)
        mem_dst = joined(stage, step, step).astype(BF16)
        mem_src_ref[pl.ds(base, step), :] = mem_src
        mem_dst_ref[pl.ds(base, step), :] = mem_dst
        rows, _, _, _, _, hidden = gru_forward(mem_src, mem_dst, w_input_ref, w_hidden_ref)
        delta[pl.ds(base, step), :] = (hidden - rows).astype(BF16)
        return carry

    lax.fori_loop(0, events // step, body, 0)
    source = src_row_ref[...]
    slot = (source >> 8) * UCAP + (source & 255)
    reps, block_width = change_ref.shape[1], change_ref.shape[3]
    slots = change_ref.shape[0] * UCAP
    part = 256
    for k in range(slots // part):
        ids = lax.broadcasted_iota(jnp.int32, (part, events), 0) + k * part
        picked = jnp.where(ids == slot, 1.0, 0.0).astype(BF16)
        block = dot(picked, delta[...]).astype(BF16).reshape(part // UCAP, 1, UCAP, block_width)
        owners = pl.ds(k * (part // UCAP), part // UCAP)
        change_ref[owners] = jnp.broadcast_to(block, (part // UCAP, reps, UCAP, block_width))


def memory_step(src_slot, dst_slot, fetched, w_input, w_hidden, reps):
    events = src_slot.shape[0]
    count, width = fetched.shape
    owners = count // 256
    return pl.pallas_call(
        memory_kernel,
        out_shape=(
            jax.ShapeDtypeStruct((events, width), BF16),
            jax.ShapeDtypeStruct((events, width), BF16),
            jax.ShapeDtypeStruct((owners, reps, UCAP, width), BF16),
        ),
        in_specs=[SMEM, SMEM, VMEM, VMEM, VMEM, VMEM],
        out_specs=(VMEM, VMEM, VMEM),
        scratch_shapes=[
            pltpu.VMEM((2 * count, 128), F32),
            pltpu.VMEM((512, 128), F32),
            pltpu.VMEM((events, width), BF16),
        ],
        compiler_params=pltpu.CompilerParams(vmem_limit_bytes=LIMIT),
        cost_estimate=cost(8),
        name="memory_step",
    )(2 * src_slot, 2 * dst_slot, src_slot.reshape(1, events), fetched, w_input, w_hidden)


COS_TERMS = (
    1.0,
    -0.49999988079071045,
    0.041666485369205475,
    -0.001388777862302959,
    2.4769342417130247e-05,
    -2.7073761543761066e-07,
    1.7225967319234314e-09,
)
TURN_HIGH = 6.28125
TURN_LOW = 2.0 * math.pi - 6.28125


def cosine(x):
    turns = jnp.floor(x * (0.5 / math.pi) + 0.5)
    rest = (x - turns * TURN_HIGH) - turns * TURN_LOW
    square = rest * rest
    total = jnp.full_like(x, COS_TERMS[-1])
    for term in COS_TERMS[-2::-1]:
        total = total * square + term
    return total


GROUP = 16


def phase_kernel(spacing_ref, freq_ref, w_time_ref, phase_ref, timed_ref):
    wave = cosine(freq_ref[...] * spacing_ref[...]).astype(BF16)
    phase_ref[...] = wave
    timed_ref[...] = dot_tn(wave, w_time_ref[...]).astype(BF16)


def phase_step(spacing, frequency, w_time):
    total = spacing.shape[1]
    freqs, width = w_time.shape
    step = 1024
    return pl.pallas_call(
        phase_kernel,
        out_shape=(
            jax.ShapeDtypeStruct((freqs, total), BF16),
            jax.ShapeDtypeStruct((total, width), BF16),
        ),
        grid=(total // step,),
        in_specs=[
            pl.BlockSpec((1, step), lambda i: (0, i)),
            pl.BlockSpec((freqs, 1), lambda i: (0, 0)),
            pl.BlockSpec((freqs, width), lambda i: (0, 0)),
        ],
        out_specs=(
            pl.BlockSpec((freqs, step), lambda i: (0, i)),
            pl.BlockSpec((step, width), lambda i: (i, 0)),
        ),
        compiler_params=pltpu.CompilerParams(vmem_limit_bytes=LIMIT),
        cost_estimate=cost(10),
        name="phase_step",
    )(spacing, frequency.reshape(freqs, 1), w_time)


def events_kernel(
    nbr_ref, rows_ref, phase_ref, timed_ref, mem_src_ref, mem_dst_ref, slope_ref,
    w_input_ref, w_hidden_ref, w_time_ref, w_query_ref, w_key_ref, w_value_ref, w_out_ref,
    grads_ref,
    rows_in, phase, timed, table, stage, ones, mixed, keys, values, score, dprob, slopes,
    hidden_half, query, dattended, reset, update, candidate, hid_c, attended, dquery,
    acc_time, acc_kv, both_weights, dmixed, row_sems, time_sems, phase_sem,
):
    events, width = slope_ref.shape
    nbrs = nbr_ref.shape[0] // events
    flat = stage.shape[0] // 2
    size = flat // nbrs
    blocks = events // size
    large = dmixed.shape[0]
    head = width // HEADS
    scale = head ** -0.5
    chunks = row_sems.shape[0]
    part = rows_in.shape[0] // chunks
    row_copies = [
        pltpu.make_async_copy(
            rows_ref.at[pl.ds(c * part, part)], rows_in.at[pl.ds(c * part, part)], row_sems.at[c]
        )
        for c in range(chunks)
    ]

    def time_copy(c):
        length = nbrs * events // time_sems.shape[0]
        span = pl.ds(pl.multiple_of(c * length, length), length)
        return pltpu.make_async_copy(timed_ref.at[span], timed.at[span], time_sems.at[c])

    for copy in row_copies:
        copy.start()
    for c in range(time_sems.shape[0]):
        time_copy(c).start()
    phase_copy = pltpu.make_async_copy(phase_ref, phase, phase_sem)
    phase_copy.start()
    row_id = lax.broadcasted_iota(jnp.int32, (width, width), 0) // head
    col_id = lax.broadcasted_iota(jnp.int32, (width, width), 1) // head
    ones[...] = jnp.where(row_id == col_id, 1.0, 0.0).astype(BF16)
    both_weights[:, :width] = w_key_ref[...]
    both_weights[:, width:] = w_value_ref[...]
    for ref in (acc_time, acc_kv):
        ref[...] = jnp.zeros_like(ref)

    def forward(i, carry):
        span = pl.ds(pl.multiple_of(i * 256, 256), 256)
        _, r, u, c, h, hidden = gru_forward(mem_src_ref[span, :], mem_dst_ref[span, :], w_input_ref, w_hidden_ref)
        reset[span, :] = r
        update[span, :] = u
        candidate[span, :] = c
        hid_c[span, :] = h
        half = hidden.astype(BF16)
        hidden_half[span, :] = half
        query[span, :] = dot(half, w_query_ref[...]).astype(BF16)
        dattended[span, :] = dot_nt(slope_ref[span, :], w_out_ref[...]).astype(BF16)
        return carry

    lax.fori_loop(0, events // 256, forward, 0)
    for c in range(chunks):
        row_copies[c].wait()
        spread_table(rows_in.at[pl.ds(c * part, part)], table, 2 * c * part, 256)
    pick_rows(nbr_ref, 0, table, stage, flat)
    def body(i, carry):
        at = pl.multiple_of(i * flat, flat)
        event = pl.multiple_of(i * size, size)
        wave_part = nbrs * events // time_sems.shape[0]

        @pl.when(lax.rem(at, wave_part) == 0)
        def _():
            time_copy(at // wave_part).wait()

        rows = (joined(stage, 0, flat) + timed[pl.ds(at, flat), :].astype(F32)).astype(BF16)
        mixed[pl.ds(at, flat), :] = rows
        key = dot(rows, w_key_ref[...]).astype(BF16)
        value = dot(rows, w_value_ref[...]).astype(BF16)
        keys[...] = key
        values[...] = value
        key_side, value_side = [], []
        for g in range(size // GROUP):
            own = pl.ds(event + g * GROUP, GROUP)
            one_query, one_slope = query[own, :], dattended[own, :]
            for j in range(nbrs):
                span = slice((g * nbrs + j) * GROUP, (g * nbrs + j + 1) * GROUP)
                key_side.append(key[span, :] * one_query)
                value_side.append(value[span, :] * one_slope)
        score[...] = dot(jnp.concatenate(key_side, axis=0), ones[...])
        dprob[...] = dot(jnp.concatenate(value_side, axis=0), ones[...])
        upcoming = jnp.minimum(i + 1, blocks - 1) * flat
        for g in range(size // GROUP):
            own = pl.ds(event + g * GROUP, GROUP)
            spans = [pl.ds((g * nbrs + j) * GROUP, GROUP) for j in range(nbrs)]
            scores = [score[span, :] for span in spans]
            top = functools.reduce(jnp.maximum, scores)
            weights = [jnp.exp2((s - top) * (scale * math.log2(math.e))) for s in scores]
            total = functools.reduce(jnp.add, weights)
            inverse = 1.0 / total
            outcome, overlap = jnp.zeros_like(top), jnp.zeros_like(top)
            for j in range(nbrs):
                outcome = outcome + weights[j] * values[spans[j], :].astype(F32)
                overlap = overlap + weights[j] * dprob[spans[j], :]
                pick_rows(nbr_ref, upcoming, table, stage, GROUP // 2, (g * nbrs + j) * GROUP)
            overlap = overlap * inverse
            attended[own, :] = (outcome * inverse).astype(BF16)
            datt = dattended[own, :].astype(F32)
            asked = query[own, :].astype(F32) * scale
            change = jnp.zeros_like(top)
            for j in range(nbrs):
                span = spans[j]
                prob = weights[j] * inverse
                dscore = prob * (dprob[span, :] - overlap)
                change = change + dscore * keys[span, :].astype(F32)
                here = pl.ds(at + (g * nbrs + j) * GROUP, GROUP)
                slopes[here, :width] = (dscore * asked).astype(BF16)
                slopes[here, width:] = (prob * datt).astype(BF16)
                pick_rows(nbr_ref, upcoming, table, stage, GROUP // 2, (g * nbrs + j) * GROUP + GROUP // 2)
            dquery[own, :] = (change * scale).astype(BF16)
        return carry

    lax.fori_loop(0, blocks, body, 0)

    phase_copy.wait()
    for i in range(nbrs * events // large):
        for k in range(large // 256):
            span = slice(i * large + k * 256, i * large + (k + 1) * 256)
            dmixed[k * 256 : (k + 1) * 256, :] = dot_nt(slopes[span, :], both_weights[...]).astype(BF16)
        span = slice(i * large, (i + 1) * large)
        acc_time[...] += dot(phase[:, span], dmixed[...])
        acc_kv[...] += dot_tn(mixed[span, :], slopes[span, :])
    total_rows = 0

    def write(value):
        nonlocal total_rows
        depth, columns = value.shape
        for k in range(columns // 128):
            grads_ref[total_rows : total_rows + depth, :] = value[:, k * 128 : (k + 1) * 128].astype(BF16)
            total_rows += depth

    mem_src, mem_dst, slope = mem_src_ref[...], mem_dst_ref[...], slope_ref[...]
    rows = mem_src.astype(F32)
    dhidden = slope.astype(F32) + dot_nt(dquery[...], w_query_ref[...])
    u, c, r = update[...], candidate[...], reset[...]
    dcand = dhidden * (1.0 - u) * (1.0 - c * c)
    dupdate = (dhidden * (rows - c) * u * (1.0 - u)).astype(BF16)
    dreset = (dcand * hid_c[...] * r * (1.0 - r)).astype(BF16)
    for piece in (dreset, dupdate, dcand.astype(BF16)):
        write(dot_tn(mem_dst, piece))
    for piece in (dreset, dupdate, (dcand * r).astype(BF16)):
        write(dot_tn(mem_src, piece))
    write(acc_time[...])
    write(dot_tn(hidden_half[...], dquery[...]))
    write(acc_kv[...])
    write(dot_tn(attended[...], slope))
    if total_rows < grads_ref.shape[0]:
        grads_ref[total_rows:, :] = jnp.zeros((grads_ref.shape[0] - total_rows, 128), BF16)


def events_step(nbr_index, fetched, phase, timed, mem_src, mem_dst, slope, weights, grad_rows, size=64):
    events, width = slope.shape
    nbrs = nbr_index.shape[0] // events
    count = fetched.shape[0]
    freqs = phase.shape[0]
    flat = nbrs * size
    anywhere = pl.BlockSpec(memory_space=pl.ANY)
    halves = pltpu.VMEM((events, width), BF16)
    wholes = pltpu.VMEM((events, width), F32)
    return pl.pallas_call(
        events_kernel,
        out_shape=jax.ShapeDtypeStruct((grad_rows, 128), BF16),
        in_specs=[SMEM, anywhere, anywhere, anywhere] + [VMEM] * 10,
        out_specs=VMEM,
        scratch_shapes=[
            pltpu.VMEM((count, width), BF16),
            pltpu.VMEM((freqs, nbrs * events), BF16),
            pltpu.VMEM((nbrs * events, width), BF16),
            pltpu.VMEM((2 * count, 128), F32),
            pltpu.VMEM((2 * flat, 128), F32),
            pltpu.VMEM((width, width), BF16),
            pltpu.VMEM((nbrs * events, width), BF16),
            pltpu.VMEM((flat, width), BF16),
            pltpu.VMEM((flat, width), BF16),
            pltpu.VMEM((flat, width), F32),
            pltpu.VMEM((flat, width), F32),
            pltpu.VMEM((nbrs * events, 2 * width), BF16),
            halves, halves, halves, wholes, wholes, wholes, wholes, halves, halves,
            pltpu.VMEM((freqs, width), F32),
            pltpu.VMEM((width, 2 * width), F32),
            pltpu.VMEM((width, 2 * width), BF16),
            pltpu.VMEM((2560, width), BF16),
            pltpu.SemaphoreType.DMA((8,)),
            pltpu.SemaphoreType.DMA((4,)),
            pltpu.SemaphoreType.DMA,
        ],
        compiler_params=pltpu.CompilerParams(vmem_limit_bytes=LIMIT),
        cost_estimate=cost(40),
        name="events_step",
    )(nbr_index, fetched, phase, timed, mem_src, mem_dst, slope, *weights)


def merge_kernel(place_ref, index_ref, change_ref, memory_ref, out_ref, table, stage):
    rows = memory_ref.shape[0]
    spread_table(memory_ref, table, 0, 256)
    step = stage.shape[0] // 2
    group = UCAP
    reps = 4
    owner_rows = change_ref.shape[0] // reps
    here = place_ref[0]

    def body(i, carry):
        base = pl.multiple_of(i * step, step)
        block = change_ref[pl.ds(base, step), :].astype(F32)
        stage[pl.ds(0, step, stride=2), :] = block[:, :128]
        stage[pl.ds(1, step, stride=2), :] = block[:, 128:]
        for g in range(step // group):
            sender = i * (step // group) + g
            first = lax.rem(here - lax.rem(sender, reps) + reps, reps) * owner_rows + sender // reps * group
            spots = [pl.ds(pl.multiple_of(index_ref[first + r], 2), 2) for r in range(group)]
            sums = [
                table[spots[r], :] + stage[2 * (g * group + r) : 2 * (g * group + r) + 2, :]
                for r in range(group)
            ]
            for r in range(group):
                table[spots[r], :] = sums[r]
        return carry

    lax.fori_loop(0, change_ref.shape[0] // step, body, 0)

    def finish(i, carry):
        base = pl.multiple_of(i * 256, 256)
        left = table[pl.ds(2 * base, 256, stride=2), :]
        right = table[pl.ds(2 * base + 1, 256, stride=2), :]
        out_ref[pl.ds(base, 256), :] = jnp.concatenate([left, right], axis=1).astype(BF16)
        return carry

    lax.fori_loop(0, rows // 256, finish, 0)


def merge(place, index, change, memory):
    rows, width = memory.shape
    return pl.pallas_call(
        merge_kernel,
        out_shape=jax.ShapeDtypeStruct((rows, width), BF16),
        in_specs=[SMEM, SMEM, VMEM, VMEM],
        out_specs=VMEM,
        scratch_shapes=[pltpu.VMEM((2 * rows, 128), F32), pltpu.VMEM((256, 128), F32)],
        compiler_params=pltpu.CompilerParams(vmem_limit_bytes=LIMIT),
        cost_estimate=cost(11),
        name="merge_rows",
    )(place, index, change, memory)


def total_kernel(parts_ref, out_ref):
    total = jnp.zeros(parts_ref.shape[1:], F32)
    for k in range(parts_ref.shape[0]):
        total = total + parts_ref[k].astype(F32)
    total = total.astype(BF16)
    for k in range(parts_ref.shape[0]):
        out_ref[k] = total


def total_parts(parts):
    return pl.pallas_call(
        total_kernel,
        out_shape=jax.ShapeDtypeStruct(parts.shape, BF16),
        in_specs=[VMEM],
        out_specs=VMEM,
        compiler_params=pltpu.CompilerParams(vmem_limit_bytes=8 * 1024 * 1024),
        cost_estimate=cost(3),
        name="total_parts",
    )(parts)


def unpack_kernel(flat_ref, *out_refs):
    row = 0
    for out_ref in out_refs:
        depth, columns = out_ref.shape
        for k in range(columns // 128):
            out_ref[:, k * 128 : (k + 1) * 128] = flat_ref[row : row + depth, :].astype(F32)
            row += depth


def unpack(flat, shapes):
    return pl.pallas_call(
        unpack_kernel,
        out_shape=tuple(jax.ShapeDtypeStruct(shape, F32) for shape in shapes),
        in_specs=[VMEM],
        out_specs=tuple(VMEM for _ in shapes),
        compiler_params=pltpu.CompilerParams(vmem_limit_bytes=12 * 1024 * 1024),
        cost_estimate=cost(3),
        name="unpack_grads",
    )(flat)


BOTH = ("node", "rep")


def local(
    memory, req_rows, src_slot, dst_slot, nbr_slot, event_time, nbr_time, frequency, emb_grad,
    w_input, w_hidden, w_time, w_query, w_key, w_value, w_out,
):
    weights = (w_input, w_hidden, w_time, w_query, w_key, w_value, w_out)
    requests = req_rows[0]
    owners, capacity = requests.shape
    width = memory.shape[1]
    reps = lax.axis_size("rep")
    doubled = lax.optimization_barrier((2 * requests).reshape(owners, capacity // 128, 128))
    asked = lax.all_to_all(doubled, "node", split_axis=0, concat_axis=0, tiled=True)
    asked = asked.reshape(owners, capacity)
    served = serve(asked.reshape(-1), memory).reshape(owners, capacity, width)
    fetched = lax.all_to_all(served, "node", split_axis=0, concat_axis=0, tiled=True)
    fetched = fetched.reshape(owners * capacity, width)
    lead = asked[:, :UCAP]
    turned = [lead] + [
        lax.ppermute(lead, "rep", [(i, (i + k) % reps) for i in range(reps)]) for k in range(1, reps)
    ]
    touched = jnp.stack(turned).reshape(-1)
    place = lax.axis_index("rep").astype(jnp.int32).reshape(1)
    events, nbrs = nbr_slot.shape
    nbr_index = (2 * nbr_slot).reshape(events // GROUP, GROUP, nbrs).transpose(0, 2, 1).reshape(-1)
    spacing = (event_time[:, None] - nbr_time).astype(F32)
    spacing = spacing.reshape(events // GROUP, GROUP, nbrs).transpose(0, 2, 1).reshape(1, -1)
    phase, timed = phase_step(spacing, frequency, w_time)
    fetched, touched, nbr_index, phase, timed = lax.optimization_barrier(
        (fetched, touched, nbr_index, phase, timed)
    )
    mem_src, mem_dst, change = memory_step(src_slot, dst_slot, fetched, w_input, w_hidden, reps)
    updates = lax.all_to_all(change.reshape(owners * reps * UCAP, width), BOTH, split_axis=0, concat_axis=0, tiled=True)
    shapes = (w_input.shape, w_hidden.shape, w_time.shape, w_query.shape, w_key.shape, w_value.shape, w_out.shape)
    used = sum(shape[0] * shape[1] for shape in shapes) // 128
    devices = owners * reps
    share = -(-used // (devices * 16)) * 16
    grads = events_step(nbr_index, fetched, phase, timed, mem_src, mem_dst, emb_grad, weights, devices * share)
    grads, updates = lax.optimization_barrier((grads, updates))
    parts = lax.all_to_all(grads, BOTH, split_axis=0, concat_axis=0, tiled=True)
    summed = total_parts(parts.reshape(devices, share, 128))
    flat = lax.all_to_all(summed.reshape(devices * share, 128), BOTH, split_axis=0, concat_axis=0, tiled=True)
    new_memory = merge(place, touched, updates, memory)
    return (new_memory, *unpack(flat, shapes))


def solution(mesh):
    split = P(BOTH)
    placed = (
        P("node", None), P(BOTH, None, None), split, split, P(BOTH, None), split, P(BOTH, None),
        P(), P(BOTH, None), P(), P(), P(), P(), P(), P(), P(),
    )
    return jax.shard_map(
        local,
        mesh=mesh,
        in_specs=placed,
        out_specs=(P("node", None), P(), P(), P(), P(), P(), P(), P()),
        check_vma=False,
    )
```

```python
import functools
import math

import jax
import jax.numpy as jnp
from jax import lax
from jax.experimental import pallas as pl
from jax.experimental.pallas import tpu as pltpu
from jax.sharding import PartitionSpec as P

HEADS = 8
UCAP = 32
F32 = jnp.float32
BF16 = jnp.bfloat16
VMEM = pl.BlockSpec(memory_space=pltpu.VMEM)
SMEM = pl.BlockSpec(memory_space=pltpu.SMEM)
LIMIT = 58 * 1024 * 1024


def cost(micros):
    return pl.CostEstimate(flops=int(micros * 1.1e9), bytes_accessed=int(micros * 3.0e6), transcendentals=0)


def dot(a, b):
    return jnp.dot(a, b, preferred_element_type=F32)


def dot_nt(a, b):
    return lax.dot_general(a, b, (((1,), (1,)), ((), ())), preferred_element_type=F32)


def dot_tn(a, b):
    return lax.dot_general(a, b, (((0,), (0,)), ((), ())), preferred_element_type=F32)


def spread_table(rows_ref, table, base, step):
    count = rows_ref.shape[0]

    def body(i, carry):
        block = rows_ref[pl.ds(pl.multiple_of(i * step, step), step), :].astype(F32)
        start = base + i * (2 * step)
        table[pl.ds(start, step, stride=2), :] = block[:, :128]
        table[pl.ds(start + 1, step, stride=2), :] = block[:, 128:]
        return carry

    lax.fori_loop(0, count // step, body, 0)


def merged(table, spots):
    sublane = lax.broadcasted_iota(jnp.int32, (8, 128), 0) // 2
    found = [table[pl.ds(spot + (8 - 2 * k), 8), :] for k, spot in enumerate(spots)]
    lower = jnp.where(sublane == 0, found[0], found[1])
    upper = jnp.where(sublane == 2, found[2], found[3])
    return jnp.where(sublane < 2, lower, upper)


def pick_pairs(index_ref, offset, table, stage, count, low, high):
    for r in range(0, count, 4):
        words = [index_ref[offset + r + k] for k in range(4)]
        stage[2 * (low + r) : 2 * (low + r) + 8, :] = merged(table, [word & 0xFFFF for word in words])
        stage[2 * (high + r) : 2 * (high + r) + 8, :] = merged(table, [word >> 16 for word in words])


def pick_rows(index_ref, offset, table, stage, count, start=0):
    for r in range(start, start + count):
        spot = index_ref[offset + r]
        stage[2 * r : 2 * r + 2, :] = table[pl.ds(pl.multiple_of(spot, 2), 2), :]


def paired(first, second):
    return (2 * first) | (second << 17)


def joined(stage, start, count):
    left = stage[pl.ds(2 * start, count, stride=2), :]
    right = stage[pl.ds(2 * start + 1, count, stride=2), :]
    return jnp.concatenate([left, right], axis=1)


def serve_kernel(index_ref, rows_ref, out_ref, table, stage):
    block = pl.program_id(0)
    step = stage.shape[0] // 2
    count = out_ref.shape[0]
    half = 128

    @pl.when(block == 0)
    def _():
        spread_table(rows_ref, table, 8, 256)

    def body(i, carry):
        base = pl.multiple_of(i * step, step)
        for k in range(step // (2 * half)):
            word = (block * count + base) // 2 + k * half
            pick_pairs(index_ref, word, table, stage, half, 2 * k * half, (2 * k + 1) * half)
        out_ref[pl.ds(base, step), :] = joined(stage, 0, step).astype(BF16)
        return carry

    lax.fori_loop(0, count // step, body, 0)


def serve(index, memory):
    count = 2 * index.shape[0]
    rows, width = memory.shape
    blocks = 4
    return pl.pallas_call(
        serve_kernel,
        out_shape=jax.ShapeDtypeStruct((count, width), BF16),
        grid=(blocks,),
        in_specs=[SMEM, VMEM],
        out_specs=pl.BlockSpec((count // blocks, width), lambda i: (i, 0)),
        scratch_shapes=[pltpu.VMEM((2 * rows + 16, 128), F32), pltpu.VMEM((2048, 128), F32)],
        compiler_params=pltpu.CompilerParams(vmem_limit_bytes=LIMIT),
        cost_estimate=cost(11),
        name="serve_rows",
    )(index, memory)


def sigmoid(x):
    return 1.0 / (1.0 + jnp.exp(-x))


def gru_forward(mem_src, mem_dst, w_input_ref, w_hidden_ref):
    width = mem_src.shape[1]
    parts_in = [dot(mem_dst, w_input_ref[:, k * width : (k + 1) * width]) for k in range(3)]
    parts_hid = [dot(mem_src, w_hidden_ref[:, k * width : (k + 1) * width]) for k in range(3)]
    reset = sigmoid(parts_in[0] + parts_hid[0])
    update = sigmoid(parts_in[1] + parts_hid[1])
    candidate = jnp.tanh(parts_in[2] + reset * parts_hid[2])
    rows = mem_src.astype(F32)
    hidden = (1.0 - update) * candidate + update * rows
    return rows, reset, update, candidate, parts_hid[2], hidden


def memory_kernel(
    pair_ref, src_row_ref, rows_ref, w_input_ref, w_hidden_ref,
    mem_src_ref, mem_dst_ref, change_ref, table, stage, delta,
):
    spread_table(rows_ref, table, 8, 256)
    step = stage.shape[0] // 4
    events = mem_src_ref.shape[0]

    def body(i, carry):
        base = pl.multiple_of(i * step, step)
        pick_pairs(pair_ref, base, table, stage, step, 0, step)
        mem_src = joined(stage, 0, step).astype(BF16)
        mem_dst = joined(stage, step, step).astype(BF16)
        mem_src_ref[pl.ds(base, step), :] = mem_src
        mem_dst_ref[pl.ds(base, step), :] = mem_dst
        rows, _, _, _, _, hidden = gru_forward(mem_src, mem_dst, w_input_ref, w_hidden_ref)
        delta[pl.ds(base, step), :] = (hidden - rows).astype(BF16)
        return carry

    lax.fori_loop(0, events // step, body, 0)
    source = src_row_ref[...]
    slot = (source >> 8) * UCAP + (source & 255)
    reps, block_width = change_ref.shape[1], change_ref.shape[3]
    slots = change_ref.shape[0] * UCAP
    part = 256
    for k in range(slots // part):
        ids = lax.broadcasted_iota(jnp.int32, (part, events), 0) + k * part
        picked = jnp.where(ids == slot, 1.0, 0.0).astype(BF16)
        block = dot(picked, delta[...]).astype(BF16).reshape(part // UCAP, 1, UCAP, block_width)
        owners = pl.ds(k * (part // UCAP), part // UCAP)
        change_ref[owners] = jnp.broadcast_to(block, (part // UCAP, reps, UCAP, block_width))


def memory_step(src_slot, dst_slot, fetched, w_input, w_hidden, reps):
    events = src_slot.shape[0]
    count, width = fetched.shape
    owners = count // 256
    return pl.pallas_call(
        memory_kernel,
        out_shape=(
            jax.ShapeDtypeStruct((events, width), BF16),
            jax.ShapeDtypeStruct((events, width), BF16),
            jax.ShapeDtypeStruct((owners, reps, UCAP, width), BF16),
        ),
        in_specs=[SMEM, VMEM, VMEM, VMEM, VMEM],
        out_specs=(VMEM, VMEM, VMEM),
        scratch_shapes=[
            pltpu.VMEM((2 * count + 16, 128), F32),
            pltpu.VMEM((1024, 128), F32),
            pltpu.VMEM((events, width), BF16),
        ],
        compiler_params=pltpu.CompilerParams(vmem_limit_bytes=LIMIT),
        cost_estimate=cost(8),
        name="memory_step",
    )(paired(src_slot, dst_slot), src_slot.reshape(1, events), fetched, w_input, w_hidden)


COS_TERMS = (
    1.0,
    -0.49999988079071045,
    0.041666485369205475,
    -0.001388777862302959,
    2.4769342417130247e-05,
    -2.7073761543761066e-07,
    1.7225967319234314e-09,
)
TURN_HIGH = 6.28125
TURN_LOW = 2.0 * math.pi - 6.28125


def cosine(x):
    turns = jnp.floor(x * (0.5 / math.pi) + 0.5)
    rest = (x - turns * TURN_HIGH) - turns * TURN_LOW
    square = rest * rest
    total = jnp.full_like(x, COS_TERMS[-1])
    for term in COS_TERMS[-2::-1]:
        total = total * square + term
    return total


GROUP = 16


def phase_kernel(spacing_ref, freq_ref, w_time_ref, phase_ref, timed_ref):
    wave = cosine(freq_ref[...] * spacing_ref[...]).astype(BF16)
    phase_ref[...] = wave
    timed_ref[...] = dot_tn(wave, w_time_ref[...]).astype(BF16)


def phase_step(spacing, frequency, w_time):
    total = spacing.shape[1]
    freqs, width = w_time.shape
    step = 1024
    return pl.pallas_call(
        phase_kernel,
        out_shape=(
            jax.ShapeDtypeStruct((freqs, total), BF16),
            jax.ShapeDtypeStruct((total, width), BF16),
        ),
        grid=(total // step,),
        in_specs=[
            pl.BlockSpec((1, step), lambda i: (0, i)),
            pl.BlockSpec((freqs, 1), lambda i: (0, 0)),
            pl.BlockSpec((freqs, width), lambda i: (0, 0)),
        ],
        out_specs=(
            pl.BlockSpec((freqs, step), lambda i: (0, i)),
            pl.BlockSpec((step, width), lambda i: (i, 0)),
        ),
        compiler_params=pltpu.CompilerParams(vmem_limit_bytes=LIMIT),
        cost_estimate=cost(10),
        name="phase_step",
    )(spacing, frequency.reshape(freqs, 1), w_time)


def pick_quads(index_ref, offset, table, stage, count, start=0):
    for r in range(start, start + count, 4):
        stage[2 * r : 2 * r + 8, :] = merged(table, [index_ref[offset + r + k] for k in range(4)])


def twice(x):
    return jnp.concatenate([x, x], axis=1)


def events_kernel(
    nbr_ref, rows_ref, phase_ref, timed_ref, mem_src_ref, mem_dst_ref, slope_ref,
    w_input_ref, w_hidden_ref, w_time_ref, w_query_ref, w_key_ref, w_value_ref, w_out_ref,
    grads_ref,
    rows_in, phase, timed, table, stage, ones, mixed, keys, values, score, dprob, slopes,
    hidden_half, query, dattended, reset, update, candidate, hid_c, attended, dquery,
    acc_time, acc_kv, both_weights, query_weights, out_weights, order, row_sems, time_sems, phase_sem,
):
    events, width = slope_ref.shape
    nbrs = nbr_ref.shape[0] // events
    flat = stage.shape[0] // 2
    size = flat // nbrs
    blocks = events // size
    large = 2560
    head = width // HEADS
    scale = head ** -0.5
    chunks = row_sems.shape[0]
    part = rows_in.shape[0] // chunks
    row_copies = [
        pltpu.make_async_copy(
            rows_ref.at[pl.ds(c * part, part)], rows_in.at[pl.ds(c * part, part)], row_sems.at[c]
        )
        for c in range(chunks)
    ]

    def time_copy(c):
        length = nbrs * events // time_sems.shape[0]
        span = pl.ds(pl.multiple_of(c * length, length), length)
        return pltpu.make_async_copy(timed_ref.at[span], timed.at[span], time_sems.at[c])

    for copy in row_copies:
        copy.start()
    for c in range(time_sems.shape[0]):
        time_copy(c).start()
    phase_copy = pltpu.make_async_copy(phase_ref, phase, phase_sem)
    phase_copy.start()
    old_column = lax.broadcasted_iota(jnp.int32, (width, width), 0)
    new_column = lax.broadcasted_iota(jnp.int32, (width, width), 1)
    lanes = width // 2
    part_head = head // 2
    moved = (new_column % lanes) // part_head * head + new_column // lanes * part_head + new_column % part_head
    order[...] = jnp.where(moved == old_column, 1.0, 0.0).astype(BF16)
    of_row = lax.broadcasted_iota(jnp.int32, (width, lanes), 0) % lanes // part_head
    of_lane = lax.broadcasted_iota(jnp.int32, (width, lanes), 1) // part_head
    ones[...] = jnp.where(of_row == of_lane, 1.0, 0.0).astype(BF16)
    query_weights[...] = dot(w_query_ref[...], order[...]).astype(BF16)
    out_weights[...] = dot_tn(order[...], w_out_ref[...]).astype(BF16)
    both_weights[:, :width] = dot(w_key_ref[...], order[...]).astype(BF16)
    both_weights[:, width:] = dot(w_value_ref[...], order[...]).astype(BF16)
    for ref in (acc_time, acc_kv):
        ref[...] = jnp.zeros_like(ref)

    def forward(i, carry):
        span = pl.ds(pl.multiple_of(i * 256, 256), 256)
        _, r, u, c, h, hidden = gru_forward(mem_src_ref[span, :], mem_dst_ref[span, :], w_input_ref, w_hidden_ref)
        reset[span, :] = r
        update[span, :] = u
        candidate[span, :] = c
        hid_c[span, :] = h
        half = hidden.astype(BF16)
        hidden_half[span, :] = half
        query[span, :] = dot(half, query_weights[...]).astype(BF16)
        dattended[span, :] = dot_nt(slope_ref[span, :], out_weights[...]).astype(BF16)
        return carry

    lax.fori_loop(0, events // 256, forward, 0)
    for c in range(chunks):
        row_copies[c].wait()
        spread_table(rows_in.at[pl.ds(c * part, part)], table, 8 + 2 * c * part, 256)
    pick_quads(nbr_ref, 0, table, stage, flat)
    def body(i, carry):
        at = pl.multiple_of(i * flat, flat)
        event = pl.multiple_of(i * size, size)
        wave_part = nbrs * events // time_sems.shape[0]

        @pl.when(lax.rem(at, wave_part) == 0)
        def _():
            time_copy(at // wave_part).wait()

        rows = (joined(stage, 0, flat) + timed[pl.ds(at, flat), :].astype(F32)).astype(BF16)
        mixed[pl.ds(at, flat), :] = rows
        key = dot(rows, both_weights[:, :width]).astype(BF16)
        value = dot(rows, both_weights[:, width:]).astype(BF16)
        keys[...] = key
        values[...] = value
        key_side, value_side = [], []
        for g in range(size // GROUP):
            own = pl.ds(event + g * GROUP, GROUP)
            one_query, one_slope = query[own, :], dattended[own, :]
            for j in range(nbrs):
                span = slice((g * nbrs + j) * GROUP, (g * nbrs + j + 1) * GROUP)
                key_side.append(key[span, :] * one_query)
                value_side.append(value[span, :] * one_slope)
        score[...] = dot(jnp.concatenate(key_side, axis=0), ones[...])
        dprob[...] = dot(jnp.concatenate(value_side, axis=0), ones[...])
        upcoming = jnp.minimum(i + 1, blocks - 1) * flat
        for g in range(size // GROUP):
            own = pl.ds(event + g * GROUP, GROUP)
            spans = [pl.ds((g * nbrs + j) * GROUP, GROUP) for j in range(nbrs)]
            scores = [score[span, :] for span in spans]
            top = functools.reduce(jnp.maximum, scores)
            weights = [jnp.exp2((s - top) * (scale * math.log2(math.e))) for s in scores]
            total = functools.reduce(jnp.add, weights)
            inverse = 1.0 / total
            outcome, overlap = jnp.zeros((GROUP, width), F32), jnp.zeros_like(top)
            for j in range(nbrs):
                outcome = outcome + twice(weights[j]) * values[spans[j], :].astype(F32)
                overlap = overlap + weights[j] * dprob[spans[j], :]
                pick_quads(nbr_ref, upcoming, table, stage, GROUP // 2, (g * nbrs + j) * GROUP)
            overlap = overlap * inverse
            attended[own, :] = (outcome * twice(inverse)).astype(BF16)
            datt = dattended[own, :].astype(F32)
            asked = query[own, :].astype(F32) * scale
            change = jnp.zeros((GROUP, width), F32)
            for j in range(nbrs):
                span = spans[j]
                prob = weights[j] * inverse
                dscore = twice(prob * (dprob[span, :] - overlap))
                change = change + dscore * keys[span, :].astype(F32)
                here = pl.ds(at + (g * nbrs + j) * GROUP, GROUP)
                slopes[here, :width] = (dscore * asked).astype(BF16)
                slopes[here, width:] = (twice(prob) * datt).astype(BF16)
                pick_quads(nbr_ref, upcoming, table, stage, GROUP // 2, (g * nbrs + j) * GROUP + GROUP // 2)
            dquery[own, :] = (change * scale).astype(BF16)
        return carry

    lax.fori_loop(0, blocks, body, 0)

    phase_copy.wait()
    for i in range(nbrs * events // large):
        span = slice(i * large, (i + 1) * large)
        acc_time[...] += dot(phase[:, span], slopes[span, :])
        acc_kv[...] += dot_tn(mixed[span, :], slopes[span, :])
    total_rows = 0
    packed_ref = grads_ref

    def write(value):
        nonlocal total_rows
        depth, columns = value.shape
        for k in range(columns // 128):
            packed_ref[total_rows : total_rows + depth, :] = value[:, k * 128 : (k + 1) * 128].astype(BF16)
            total_rows += depth

    mem_src, mem_dst, slope = mem_src_ref[...], mem_dst_ref[...], slope_ref[...]
    rows = mem_src.astype(F32)
    dhidden = slope.astype(F32) + dot_nt(dquery[...], query_weights[...])
    u, c, r = update[...], candidate[...], reset[...]
    dcand = dhidden * (1.0 - u) * (1.0 - c * c)
    dupdate = (dhidden * (rows - c) * u * (1.0 - u)).astype(BF16)
    dreset = (dcand * hid_c[...] * r * (1.0 - r)).astype(BF16)
    for piece in (dreset, dupdate, dcand.astype(BF16)):
        write(dot_tn(mem_dst, piece))
    for piece in (dreset, dupdate, (dcand * r).astype(BF16)):
        write(dot_tn(mem_src, piece))
    time_high = acc_time[...].astype(BF16)
    time_low = (acc_time[...] - time_high.astype(F32)).astype(BF16)
    write(dot_nt(time_high, both_weights[...]) + dot_nt(time_low, both_weights[...]))
    write(dot_nt(dot_tn(hidden_half[...], dquery[...]).astype(BF16), order[...]))
    write(dot_nt(acc_kv[:, :width].astype(BF16), order[...]))
    write(dot_nt(acc_kv[:, width:].astype(BF16), order[...]))
    write(dot(order[...], dot_tn(attended[...], slope).astype(BF16)))


def events_step(nbr_index, fetched, phase, timed, mem_src, mem_dst, slope, weights, grad_rows, size=128):
    events, width = slope.shape
    nbrs = nbr_index.shape[0] // events
    count = fetched.shape[0]
    freqs = phase.shape[0]
    flat = nbrs * size
    anywhere = pl.BlockSpec(memory_space=pl.ANY)
    halves = pltpu.VMEM((events, width), BF16)
    wholes = pltpu.VMEM((events, width), F32)
    return pl.pallas_call(
        events_kernel,
        out_shape=jax.ShapeDtypeStruct((grad_rows, 128), BF16),
        in_specs=[SMEM, anywhere, anywhere, anywhere] + [VMEM] * 10,
        out_specs=VMEM,
        scratch_shapes=[
            pltpu.VMEM((count, width), BF16),
            pltpu.VMEM((freqs, nbrs * events), BF16),
            pltpu.VMEM((nbrs * events, width), BF16),
            pltpu.VMEM((2 * count + 16, 128), F32),
            pltpu.VMEM((2 * flat, 128), F32),
            pltpu.VMEM((width, width // 2), BF16),
            pltpu.VMEM((nbrs * events, width), BF16),
            pltpu.VMEM((flat, width), BF16),
            pltpu.VMEM((flat, width), BF16),
            pltpu.VMEM((flat, width // 2), F32),
            pltpu.VMEM((flat, width // 2), F32),
            pltpu.VMEM((nbrs * events, 2 * width), BF16),
            halves, halves, halves, wholes, wholes, wholes, wholes, halves, halves,
            pltpu.VMEM((freqs, 2 * width), F32),
            pltpu.VMEM((width, 2 * width), F32),
            pltpu.VMEM((width, 2 * width), BF16),
            pltpu.VMEM((width, width), BF16),
            pltpu.VMEM((width, width), BF16),
            pltpu.VMEM((width, width), BF16),
            pltpu.SemaphoreType.DMA((8,)),
            pltpu.SemaphoreType.DMA((4,)),
            pltpu.SemaphoreType.DMA,
        ],
        compiler_params=pltpu.CompilerParams(vmem_limit_bytes=54 * 1024 * 1024),
        cost_estimate=cost(40),
        name="events_step",
    )(nbr_index, fetched, phase, timed, mem_src, mem_dst, slope, *weights)


def merge_kernel(place_ref, index_ref, change_ref, memory_ref, out_ref, table, stage):
    rows = memory_ref.shape[0]
    spread_table(memory_ref, table, 0, 256)
    step = stage.shape[0] // 2
    group = UCAP
    reps = 4
    owner_rows = change_ref.shape[0] // reps
    here = place_ref[0]

    def body(i, carry):
        base = pl.multiple_of(i * step, step)
        block = change_ref[pl.ds(base, step), :].astype(F32)
        stage[pl.ds(0, step, stride=2), :] = block[:, :128]
        stage[pl.ds(1, step, stride=2), :] = block[:, 128:]
        for g in range(step // group):
            sender = i * (step // group) + g
            first = lax.rem(here - lax.rem(sender, reps) + reps, reps) * owner_rows + sender // reps * group
            spots = [pl.ds(pl.multiple_of(index_ref[first + r], 2), 2) for r in range(group)]
            sums = [
                table[spots[r], :] + stage[2 * (g * group + r) : 2 * (g * group + r) + 2, :]
                for r in range(group)
            ]
            for r in range(group):
                table[spots[r], :] = sums[r]
        return carry

    lax.fori_loop(0, change_ref.shape[0] // step, body, 0)

    def finish(i, carry):
        base = pl.multiple_of(i * 256, 256)
        left = table[pl.ds(2 * base, 256, stride=2), :]
        right = table[pl.ds(2 * base + 1, 256, stride=2), :]
        out_ref[pl.ds(base, 256), :] = jnp.concatenate([left, right], axis=1).astype(BF16)
        return carry

    lax.fori_loop(0, rows // 256, finish, 0)


def merge(place, index, change, memory):
    rows, width = memory.shape
    return pl.pallas_call(
        merge_kernel,
        out_shape=jax.ShapeDtypeStruct((rows, width), BF16),
        in_specs=[SMEM, SMEM, VMEM, VMEM],
        out_specs=VMEM,
        scratch_shapes=[pltpu.VMEM((2 * rows, 128), F32), pltpu.VMEM((256, 128), F32)],
        compiler_params=pltpu.CompilerParams(vmem_limit_bytes=LIMIT),
        cost_estimate=cost(11),
        name="merge_rows",
    )(place, index, change, memory)


TILE = 8


def total_kernel(parts_ref, out_ref, spread):
    share = spread.shape[0] // TILE
    parts, out = parts_ref, out_ref
    group = spread.shape[0]
    total = jnp.zeros((group, 128), F32)
    for k in range(parts.shape[0] // group):
        total = total + parts[k * group : (k + 1) * group, :].astype(F32)
    one = total[:share]
    for k in range(1, TILE):
        one = one + total[k * share : (k + 1) * share]
    for k in range(TILE):
        spread[k * share : (k + 1) * share, :] = one
    whole = spread[...].astype(BF16)
    for k in range(parts.shape[0] // group):
        out[k * group : (k + 1) * group, :] = whole


def total_parts(parts, share):
    return pl.pallas_call(
        total_kernel,
        out_shape=jax.ShapeDtypeStruct(parts.shape, BF16),
        in_specs=[VMEM],
        out_specs=VMEM,
        scratch_shapes=[pltpu.VMEM((TILE * share, 128), F32)],
        compiler_params=pltpu.CompilerParams(vmem_limit_bytes=8 * 1024 * 1024),
        cost_estimate=cost(3),
        name="total_parts",
    )(parts)


def unpack_kernel(packed_ref, *out_refs):
    flat_ref = packed_ref
    row = 0
    for out_ref in out_refs:
        depth, columns = out_ref.shape
        for k in range(columns // 128):
            out_ref[:, k * 128 : (k + 1) * 128] = flat_ref[row : row + depth, :].astype(F32)
            row += depth


def unpack(flat, shapes):
    return pl.pallas_call(
        unpack_kernel,
        out_shape=tuple(jax.ShapeDtypeStruct(shape, F32) for shape in shapes),
        in_specs=[VMEM],
        out_specs=tuple(VMEM for _ in shapes),
        compiler_params=pltpu.CompilerParams(vmem_limit_bytes=12 * 1024 * 1024),
        cost_estimate=cost(3),
        name="unpack_grads",
    )(flat)


BOTH = ("node", "rep")


def exchange(rows):
    pairs = lax.optimization_barrier(rows.reshape(rows.shape[0] // 2, 2, 128))
    pairs = lax.all_to_all(pairs, BOTH, split_axis=0, concat_axis=0, tiled=True)
    return lax.optimization_barrier(pairs).reshape(rows.shape)


def local(
    memory, req_rows, src_slot, dst_slot, nbr_slot, event_time, nbr_time, frequency, emb_grad,
    w_input, w_hidden, w_time, w_query, w_key, w_value, w_out,
):
    weights = (w_input, w_hidden, w_time, w_query, w_key, w_value, w_out)
    requests = req_rows[0]
    owners, capacity = requests.shape
    width = memory.shape[1]
    reps = lax.axis_size("rep")
    half = capacity // 2
    words = lax.optimization_barrier(paired(requests[:, :half], requests[:, half:]).reshape(owners, 1, half))
    asked = lax.all_to_all(words, "node", split_axis=0, concat_axis=0, tiled=True)
    asked = asked.reshape(owners, half)
    served = serve(asked.reshape(-1), memory).reshape(owners, capacity, width)
    fetched = lax.all_to_all(served, "node", split_axis=0, concat_axis=0, tiled=True)
    fetched = fetched.reshape(owners * capacity, width)
    lead = asked[:, :UCAP] & 0xFFFF
    turned = [lead] + [
        lax.ppermute(lead, "rep", [(i, (i + k) % reps) for i in range(reps)]) for k in range(1, reps)
    ]
    touched = jnp.stack(turned).reshape(-1)
    place = lax.axis_index("rep").astype(jnp.int32).reshape(1)
    events, nbrs = nbr_slot.shape
    nbr_index = (2 * nbr_slot).reshape(events // GROUP, GROUP, nbrs).transpose(0, 2, 1).reshape(-1)
    spacing = (event_time[:, None] - nbr_time).astype(F32)
    spacing = spacing.reshape(events // GROUP, GROUP, nbrs).transpose(0, 2, 1).reshape(1, -1)
    phase, timed = phase_step(spacing, frequency, w_time)
    fetched, touched, nbr_index, phase, timed = lax.optimization_barrier(
        (fetched, touched, nbr_index, phase, timed)
    )
    mem_src, mem_dst, change = memory_step(src_slot, dst_slot, fetched, w_input, w_hidden, reps)
    updates = lax.all_to_all(change.reshape(owners * reps * UCAP, width), BOTH, split_axis=0, concat_axis=0, tiled=True)
    shapes = (w_input.shape, w_hidden.shape, w_time.shape, w_query.shape, w_key.shape, w_value.shape, w_out.shape)
    used = sum(shape[0] * shape[1] for shape in shapes) // 128
    devices = owners * reps
    share = used // devices
    grads = events_step(nbr_index, fetched, phase, timed, mem_src, mem_dst, emb_grad, weights, devices * share)
    grads, updates = lax.optimization_barrier((grads, updates))
    parts = exchange(grads)
    summed = total_parts(parts, share)
    flat = exchange(summed)
    new_memory = merge(place, touched, updates, memory)
    return (new_memory, *unpack(flat, shapes))


def solution(mesh):
    split = P(BOTH)
    placed = (
        P("node", None), P(BOTH, None, None), split, split, P(BOTH, None), split, P(BOTH, None),
        P(), P(BOTH, None), P(), P(), P(), P(), P(), P(), P(),
    )
    return jax.shard_map(
        local,
        mesh=mesh,
        in_specs=placed,
        out_specs=(P("node", None), P(), P(), P(), P(), P(), P(), P()),
        check_vma=False,
    )
```

```python
import functools
import math

import jax
import jax.numpy as jnp
from jax import lax
from jax.experimental import pallas as pl
from jax.experimental.pallas import tpu as pltpu
from jax.sharding import PartitionSpec as P

HEADS = 8
UCAP = 32
F32 = jnp.float32
BF16 = jnp.bfloat16
VMEM = pl.BlockSpec(memory_space=pltpu.VMEM)
SMEM = pl.BlockSpec(memory_space=pltpu.SMEM)
LIMIT = 58 * 1024 * 1024


def cost(micros):
    return pl.CostEstimate(flops=int(micros * 1.1e9), bytes_accessed=int(micros * 3.0e6), transcendentals=0)


def dot(a, b):
    return jnp.dot(a, b, preferred_element_type=F32)


def dot_nt(a, b):
    return lax.dot_general(a, b, (((1,), (1,)), ((), ())), preferred_element_type=F32)


def dot_tn(a, b):
    return lax.dot_general(a, b, (((0,), (0,)), ((), ())), preferred_element_type=F32)


def spread_table(rows_ref, table, base, step):
    count = rows_ref.shape[0]

    def body(i, carry):
        block = rows_ref[pl.ds(pl.multiple_of(i * step, step), step), :].astype(F32)
        start = base + i * (2 * step)
        table[pl.ds(start, step, stride=2), :] = block[:, :128]
        table[pl.ds(start + 1, step, stride=2), :] = block[:, 128:]
        return carry

    lax.fori_loop(0, count // step, body, 0)


def merged(table, spots):
    sublane = lax.broadcasted_iota(jnp.int32, (8, 128), 0) // 2
    found = [table[pl.ds(spot + (8 - 2 * k), 8), :] for k, spot in enumerate(spots)]
    lower = jnp.where(sublane == 0, found[0], found[1])
    upper = jnp.where(sublane == 2, found[2], found[3])
    return jnp.where(sublane < 2, lower, upper)


def pick_pairs(index_ref, offset, table, stage, count, low, high):
    for r in range(0, count, 4):
        words = [index_ref[offset + r + k] for k in range(4)]
        stage[2 * (low + r) : 2 * (low + r) + 8, :] = merged(table, [word & 0xFFFF for word in words])
        stage[2 * (high + r) : 2 * (high + r) + 8, :] = merged(table, [word >> 16 for word in words])


def pick_rows(index_ref, offset, table, stage, count, start=0):
    for r in range(start, start + count):
        spot = index_ref[offset + r]
        stage[2 * r : 2 * r + 2, :] = table[pl.ds(pl.multiple_of(spot, 2), 2), :]


def paired(first, second):
    return (2 * first) | (second << 17)


def joined(stage, start, count):
    left = stage[pl.ds(2 * start, count, stride=2), :]
    right = stage[pl.ds(2 * start + 1, count, stride=2), :]
    return jnp.concatenate([left, right], axis=1)


def serve_kernel(index_ref, rows_ref, out_ref, table, stage):
    block = pl.program_id(0)
    step = stage.shape[0] // 2
    count = out_ref.shape[0]
    half = 128

    @pl.when(block == 0)
    def _():
        spread_table(rows_ref, table, 8, 256)

    def body(i, carry):
        base = pl.multiple_of(i * step, step)
        for k in range(step // (2 * half)):
            word = (block * count + base) // 2 + k * half
            pick_pairs(index_ref, word, table, stage, half, 2 * k * half, (2 * k + 1) * half)
        out_ref[pl.ds(base, step), :] = joined(stage, 0, step).astype(BF16)
        return carry

    lax.fori_loop(0, count // step, body, 0)


def serve(index, memory):
    count = 2 * index.shape[0]
    rows, width = memory.shape
    blocks = 4
    return pl.pallas_call(
        serve_kernel,
        out_shape=jax.ShapeDtypeStruct((count, width), BF16),
        grid=(blocks,),
        in_specs=[SMEM, VMEM],
        out_specs=pl.BlockSpec((count // blocks, width), lambda i: (i, 0)),
        scratch_shapes=[pltpu.VMEM((2 * rows + 16, 128), F32), pltpu.VMEM((2048, 128), F32)],
        compiler_params=pltpu.CompilerParams(vmem_limit_bytes=LIMIT),
        cost_estimate=cost(11),
        name="serve_rows",
    )(index, memory)


def sigmoid(x):
    return 1.0 / (1.0 + jnp.exp(-x))


def gru_forward(mem_src, mem_dst, w_input_ref, w_hidden_ref):
    width = mem_src.shape[1]
    parts_in = [dot(mem_dst, w_input_ref[:, k * width : (k + 1) * width]) for k in range(3)]
    parts_hid = [dot(mem_src, w_hidden_ref[:, k * width : (k + 1) * width]) for k in range(3)]
    reset = sigmoid(parts_in[0] + parts_hid[0])
    update = sigmoid(parts_in[1] + parts_hid[1])
    candidate = jnp.tanh(parts_in[2] + reset * parts_hid[2])
    rows = mem_src.astype(F32)
    hidden = (1.0 - update) * candidate + update * rows
    return rows, reset, update, candidate, parts_hid[2], hidden


def memory_kernel(
    pair_ref, src_row_ref, rows_ref, w_input_ref, w_hidden_ref,
    mem_src_ref, mem_dst_ref, change_ref, table, stage, delta,
):
    spread_table(rows_ref, table, 8, 256)
    step = stage.shape[0] // 4
    events = mem_src_ref.shape[0]

    def body(i, carry):
        base = pl.multiple_of(i * step, step)
        pick_pairs(pair_ref, base, table, stage, step, 0, step)
        mem_src = joined(stage, 0, step).astype(BF16)
        mem_dst = joined(stage, step, step).astype(BF16)
        mem_src_ref[pl.ds(base, step), :] = mem_src
        mem_dst_ref[pl.ds(base, step), :] = mem_dst
        rows, _, _, _, _, hidden = gru_forward(mem_src, mem_dst, w_input_ref, w_hidden_ref)
        delta[pl.ds(base, step), :] = (hidden - rows).astype(BF16)
        return carry

    lax.fori_loop(0, events // step, body, 0)
    source = src_row_ref[...]
    slot = (source >> 8) * UCAP + (source & 255)
    reps, block_width = change_ref.shape[1], change_ref.shape[3]
    slots = change_ref.shape[0] * UCAP
    part = 256
    for k in range(slots // part):
        ids = lax.broadcasted_iota(jnp.int32, (part, events), 0) + k * part
        picked = jnp.where(ids == slot, 1.0, 0.0).astype(BF16)
        block = dot(picked, delta[...]).astype(BF16).reshape(part // UCAP, 1, UCAP, block_width)
        owners = pl.ds(k * (part // UCAP), part // UCAP)
        change_ref[owners] = jnp.broadcast_to(block, (part // UCAP, reps, UCAP, block_width))


def memory_step(src_slot, dst_slot, fetched, w_input, w_hidden, reps):
    events = src_slot.shape[0]
    count, width = fetched.shape
    owners = count // 256
    return pl.pallas_call(
        memory_kernel,
        out_shape=(
            jax.ShapeDtypeStruct((events, width), BF16),
            jax.ShapeDtypeStruct((events, width), BF16),
            jax.ShapeDtypeStruct((owners, reps, UCAP, width), BF16),
        ),
        in_specs=[SMEM, VMEM, VMEM, VMEM, VMEM],
        out_specs=(VMEM, VMEM, VMEM),
        scratch_shapes=[
            pltpu.VMEM((2 * count + 16, 128), F32),
            pltpu.VMEM((1024, 128), F32),
            pltpu.VMEM((events, width), BF16),
        ],
        compiler_params=pltpu.CompilerParams(vmem_limit_bytes=LIMIT),
        cost_estimate=cost(8),
        name="memory_step",
    )(paired(src_slot, dst_slot), src_slot.reshape(1, events), fetched, w_input, w_hidden)


COS_TERMS = (
    1.0,
    -0.49999988079071045,
    0.041666485369205475,
    -0.001388777862302959,
    2.4769342417130247e-05,
    -2.7073761543761066e-07,
    1.7225967319234314e-09,
)
TURN_HIGH = 6.28125
TURN_LOW = 2.0 * math.pi - 6.28125


def cosine(x):
    turns = jnp.floor(x * (0.5 / math.pi) + 0.5)
    rest = (x - turns * TURN_HIGH) - turns * TURN_LOW
    square = rest * rest
    total = jnp.full_like(x, COS_TERMS[-1])
    for term in COS_TERMS[-2::-1]:
        total = total * square + term
    return total


GROUP = 16


def phase_kernel(spacing_ref, freq_ref, w_time_ref, phase_ref, timed_ref):
    wave = cosine(freq_ref[...] * spacing_ref[...]).astype(BF16)
    phase_ref[...] = wave
    timed_ref[...] = dot_tn(wave, w_time_ref[...]).astype(BF16)


def phase_step(spacing, frequency, w_time):
    total = spacing.shape[1]
    freqs, width = w_time.shape
    step = 1024
    return pl.pallas_call(
        phase_kernel,
        out_shape=(
            jax.ShapeDtypeStruct((freqs, total), BF16),
            jax.ShapeDtypeStruct((total, width), BF16),
        ),
        grid=(total // step,),
        in_specs=[
            pl.BlockSpec((1, step), lambda i: (0, i)),
            pl.BlockSpec((freqs, 1), lambda i: (0, 0)),
            pl.BlockSpec((freqs, width), lambda i: (0, 0)),
        ],
        out_specs=(
            pl.BlockSpec((freqs, step), lambda i: (0, i)),
            pl.BlockSpec((step, width), lambda i: (i, 0)),
        ),
        compiler_params=pltpu.CompilerParams(vmem_limit_bytes=LIMIT),
        cost_estimate=cost(10),
        name="phase_step",
    )(spacing, frequency.reshape(freqs, 1), w_time)


def pick_quads(index_ref, offset, table, stage, count, start=0):
    for r in range(start, start + count, 4):
        stage[2 * r : 2 * r + 8, :] = merged(table, [index_ref[offset + r + k] for k in range(4)])


def twice(x):
    return jnp.concatenate([x, x], axis=1)


def events_kernel(
    nbr_ref, rows_ref, phase_ref, timed_ref, mem_src_ref, mem_dst_ref, slope_ref,
    w_input_ref, w_hidden_ref, w_time_ref, w_query_ref, w_key_ref, w_value_ref, w_out_ref,
    grads_ref,
    rows_in, phase, timed, table, stage, ones, mixed, keys, values, score, dprob, slopes,
    hidden_half, query, dattended, reset, update, candidate, hid_c, attended, dquery,
    acc_time, acc_kv, both_weights, query_weights, out_weights, order, row_sems, time_sems, phase_sem,
):
    events, width = slope_ref.shape
    nbrs = nbr_ref.shape[0] // events
    flat = stage.shape[0] // 2
    size = flat // nbrs
    blocks = events // size
    large = 2560
    head = width // HEADS
    scale = head ** -0.5
    chunks = row_sems.shape[0]
    part = rows_in.shape[0] // chunks
    row_copies = [
        pltpu.make_async_copy(
            rows_ref.at[pl.ds(c * part, part)], rows_in.at[pl.ds(c * part, part)], row_sems.at[c]
        )
        for c in range(chunks)
    ]

    def time_copy(c):
        length = nbrs * events // time_sems.shape[0]
        span = pl.ds(pl.multiple_of(c * length, length), length)
        return pltpu.make_async_copy(timed_ref.at[span], timed.at[span], time_sems.at[c])

    for copy in row_copies:
        copy.start()
    for c in range(time_sems.shape[0]):
        time_copy(c).start()
    phase_copy = pltpu.make_async_copy(phase_ref, phase, phase_sem)
    phase_copy.start()
    old_column = lax.broadcasted_iota(jnp.int32, (width, width), 0)
    new_column = lax.broadcasted_iota(jnp.int32, (width, width), 1)
    lanes = width // 2
    part_head = head // 2
    moved = (new_column % lanes) // part_head * head + new_column // lanes * part_head + new_column % part_head
    order[...] = jnp.where(moved == old_column, 1.0, 0.0).astype(BF16)
    of_row = lax.broadcasted_iota(jnp.int32, (width, lanes), 0) % lanes // part_head
    of_lane = lax.broadcasted_iota(jnp.int32, (width, lanes), 1) // part_head
    ones[...] = jnp.where(of_row == of_lane, 1.0, 0.0).astype(BF16)
    query_weights[...] = dot(w_query_ref[...], order[...]).astype(BF16)
    out_weights[...] = dot_tn(order[...], w_out_ref[...]).astype(BF16)
    both_weights[:, :width] = dot(w_key_ref[...], order[...]).astype(BF16)
    both_weights[:, width:] = dot(w_value_ref[...], order[...]).astype(BF16)
    for ref in (acc_time, acc_kv):
        ref[...] = jnp.zeros_like(ref)

    def forward(i, carry):
        span = pl.ds(pl.multiple_of(i * 256, 256), 256)
        _, r, u, c, h, hidden = gru_forward(mem_src_ref[span, :], mem_dst_ref[span, :], w_input_ref, w_hidden_ref)
        reset[span, :] = r
        update[span, :] = u
        candidate[span, :] = c
        hid_c[span, :] = h
        half = hidden.astype(BF16)
        hidden_half[span, :] = half
        query[span, :] = dot(half, query_weights[...]).astype(BF16)
        dattended[span, :] = dot_nt(slope_ref[span, :], out_weights[...]).astype(BF16)
        return carry

    lax.fori_loop(0, events // 256, forward, 0)
    for c in range(chunks):
        row_copies[c].wait()
        spread_table(rows_in.at[pl.ds(c * part, part)], table, 8 + 2 * c * part, 256)
    pick_quads(nbr_ref, 0, table, stage, flat)
    def body(i, carry):
        at = pl.multiple_of(i * flat, flat)
        event = pl.multiple_of(i * size, size)
        wave_part = nbrs * events // time_sems.shape[0]

        @pl.when(lax.rem(at, wave_part) == 0)
        def _():
            time_copy(at // wave_part).wait()

        rows = (joined(stage, 0, flat) + timed[pl.ds(at, flat), :].astype(F32)).astype(BF16)
        mixed[pl.ds(at, flat), :] = rows
        key = dot(rows, both_weights[:, :width]).astype(BF16)
        value = dot(rows, both_weights[:, width:]).astype(BF16)
        keys[...] = key
        values[...] = value
        key_side, value_side = [], []
        for g in range(size // GROUP):
            own = pl.ds(event + g * GROUP, GROUP)
            one_query, one_slope = query[own, :], dattended[own, :]
            for j in range(nbrs):
                span = slice((g * nbrs + j) * GROUP, (g * nbrs + j + 1) * GROUP)
                key_side.append(key[span, :] * one_query)
                value_side.append(value[span, :] * one_slope)
        score[...] = dot(jnp.concatenate(key_side, axis=0), ones[...])
        dprob[...] = dot(jnp.concatenate(value_side, axis=0), ones[...])
        upcoming = jnp.minimum(i + 1, blocks - 1) * flat
        for g in range(size // GROUP):
            own = pl.ds(event + g * GROUP, GROUP)
            spans = [pl.ds((g * nbrs + j) * GROUP, GROUP) for j in range(nbrs)]
            scores = [score[span, :] for span in spans]
            top = functools.reduce(jnp.maximum, scores)
            weights = [jnp.exp2((s - top) * (scale * math.log2(math.e))) for s in scores]
            total = functools.reduce(jnp.add, weights)
            inverse = 1.0 / total
            outcome, overlap = jnp.zeros((GROUP, width), F32), jnp.zeros_like(top)
            for j in range(nbrs):
                outcome = outcome + twice(weights[j]) * values[spans[j], :].astype(F32)
                overlap = overlap + weights[j] * dprob[spans[j], :]
                pick_quads(nbr_ref, upcoming, table, stage, GROUP // 2, (g * nbrs + j) * GROUP)
            overlap = overlap * inverse
            attended[own, :] = (outcome * twice(inverse)).astype(BF16)
            datt = dattended[own, :]
            asked = query[own, :]
            change = jnp.zeros((GROUP, width), F32)
            for j in range(nbrs):
                span = spans[j]
                prob = weights[j] * inverse
                dscore = twice((prob * (dprob[span, :] - overlap)) * scale)
                change = change + dscore * keys[span, :].astype(F32)
                here = pl.ds(at + (g * nbrs + j) * GROUP, GROUP)
                slopes[here, :width] = dscore.astype(BF16) * asked
                slopes[here, width:] = twice(prob.astype(BF16)) * datt
                pick_quads(nbr_ref, upcoming, table, stage, GROUP // 2, (g * nbrs + j) * GROUP + GROUP // 2)
            dquery[own, :] = change.astype(BF16)
        return carry

    lax.fori_loop(0, blocks, body, 0)

    phase_copy.wait()
    for i in range(nbrs * events // large):
        span = slice(i * large, (i + 1) * large)
        acc_time[...] += dot(phase[:, span], slopes[span, :])
        acc_kv[...] += dot_tn(mixed[span, :], slopes[span, :])
    total_rows = 0
    packed_ref = grads_ref

    def write(value):
        nonlocal total_rows
        depth, columns = value.shape
        for k in range(columns // 128):
            packed_ref[total_rows : total_rows + depth, :] = value[:, k * 128 : (k + 1) * 128].astype(BF16)
            total_rows += depth

    mem_src, mem_dst, slope = mem_src_ref[...], mem_dst_ref[...], slope_ref[...]
    rows = mem_src.astype(F32)
    dhidden = slope.astype(F32) + dot_nt(dquery[...], query_weights[...])
    u, c, r = update[...], candidate[...], reset[...]
    dcand = dhidden * (1.0 - u) * (1.0 - c * c)
    dupdate = (dhidden * (rows - c) * u * (1.0 - u)).astype(BF16)
    dreset = (dcand * hid_c[...] * r * (1.0 - r)).astype(BF16)
    for piece in (dreset, dupdate, dcand.astype(BF16)):
        write(dot_tn(mem_dst, piece))
    for piece in (dreset, dupdate, (dcand * r).astype(BF16)):
        write(dot_tn(mem_src, piece))
    time_high = acc_time[...].astype(BF16)
    time_low = (acc_time[...] - time_high.astype(F32)).astype(BF16)
    write(dot_nt(time_high, both_weights[...]) + dot_nt(time_low, both_weights[...]))
    write(dot_nt(dot_tn(hidden_half[...], dquery[...]).astype(BF16), order[...]))
    write(dot_nt(acc_kv[:, :width].astype(BF16), order[...]))
    write(dot_nt(acc_kv[:, width:].astype(BF16), order[...]))
    write(dot(order[...], dot_tn(attended[...], slope).astype(BF16)))


def events_step(nbr_index, fetched, phase, timed, mem_src, mem_dst, slope, weights, grad_rows, size=128):
    events, width = slope.shape
    nbrs = nbr_index.shape[0] // events
    count = fetched.shape[0]
    freqs = phase.shape[0]
    flat = nbrs * size
    anywhere = pl.BlockSpec(memory_space=pl.ANY)
    halves = pltpu.VMEM((events, width), BF16)
    wholes = pltpu.VMEM((events, width), F32)
    return pl.pallas_call(
        events_kernel,
        out_shape=jax.ShapeDtypeStruct((grad_rows, 128), BF16),
        in_specs=[SMEM, anywhere, anywhere, anywhere] + [VMEM] * 10,
        out_specs=VMEM,
        scratch_shapes=[
            pltpu.VMEM((count, width), BF16),
            pltpu.VMEM((freqs, nbrs * events), BF16),
            pltpu.VMEM((nbrs * events, width), BF16),
            pltpu.VMEM((2 * count + 16, 128), F32),
            pltpu.VMEM((2 * flat, 128), F32),
            pltpu.VMEM((width, width // 2), BF16),
            pltpu.VMEM((nbrs * events, width), BF16),
            pltpu.VMEM((flat, width), BF16),
            pltpu.VMEM((flat, width), BF16),
            pltpu.VMEM((flat, width // 2), F32),
            pltpu.VMEM((flat, width // 2), F32),
            pltpu.VMEM((nbrs * events, 2 * width), BF16),
            halves, halves, halves, wholes, wholes, wholes, wholes, halves, halves,
            pltpu.VMEM((freqs, 2 * width), F32),
            pltpu.VMEM((width, 2 * width), F32),
            pltpu.VMEM((width, 2 * width), BF16),
            pltpu.VMEM((width, width), BF16),
            pltpu.VMEM((width, width), BF16),
            pltpu.VMEM((width, width), BF16),
            pltpu.SemaphoreType.DMA((8,)),
            pltpu.SemaphoreType.DMA((4,)),
            pltpu.SemaphoreType.DMA,
        ],
        compiler_params=pltpu.CompilerParams(vmem_limit_bytes=54 * 1024 * 1024),
        cost_estimate=cost(40),
        name="events_step",
    )(nbr_index, fetched, phase, timed, mem_src, mem_dst, slope, *weights)


def merge_kernel(place_ref, index_ref, change_ref, memory_ref, out_ref, table, stage):
    rows = memory_ref.shape[0]
    spread_table(memory_ref, table, 0, 256)
    step = stage.shape[0] // 2
    group = UCAP
    reps = 4
    owner_rows = change_ref.shape[0] // reps
    here = place_ref[0]

    def body(i, carry):
        base = pl.multiple_of(i * step, step)
        block = change_ref[pl.ds(base, step), :].astype(F32)
        stage[pl.ds(0, step, stride=2), :] = block[:, :128]
        stage[pl.ds(1, step, stride=2), :] = block[:, 128:]
        for g in range(step // group):
            sender = i * (step // group) + g
            first = lax.rem(here - lax.rem(sender, reps) + reps, reps) * owner_rows + sender // reps * group
            spots = [pl.ds(pl.multiple_of(index_ref[first + r], 2), 2) for r in range(group)]
            sums = [
                table[spots[r], :] + stage[2 * (g * group + r) : 2 * (g * group + r) + 2, :]
                for r in range(group)
            ]
            for r in range(group):
                table[spots[r], :] = sums[r]
        return carry

    lax.fori_loop(0, change_ref.shape[0] // step, body, 0)

    def finish(i, carry):
        base = pl.multiple_of(i * 256, 256)
        left = table[pl.ds(2 * base, 256, stride=2), :]
        right = table[pl.ds(2 * base + 1, 256, stride=2), :]
        out_ref[pl.ds(base, 256), :] = jnp.concatenate([left, right], axis=1).astype(BF16)
        return carry

    lax.fori_loop(0, rows // 256, finish, 0)


def merge(place, index, change, memory):
    rows, width = memory.shape
    return pl.pallas_call(
        merge_kernel,
        out_shape=jax.ShapeDtypeStruct((rows, width), BF16),
        in_specs=[SMEM, SMEM, VMEM, VMEM],
        out_specs=VMEM,
        scratch_shapes=[pltpu.VMEM((2 * rows, 128), F32), pltpu.VMEM((256, 128), F32)],
        compiler_params=pltpu.CompilerParams(vmem_limit_bytes=LIMIT),
        cost_estimate=cost(11),
        name="merge_rows",
    )(place, index, change, memory)


TILE = 8


def total_kernel(parts_ref, out_ref, spread):
    share = spread.shape[0] // TILE
    parts, out = parts_ref, out_ref
    group = spread.shape[0]
    total = jnp.zeros((group, 128), F32)
    for k in range(parts.shape[0] // group):
        total = total + parts[k * group : (k + 1) * group, :].astype(F32)
    one = total[:share]
    for k in range(1, TILE):
        one = one + total[k * share : (k + 1) * share]
    for k in range(TILE):
        spread[k * share : (k + 1) * share, :] = one
    whole = spread[...].astype(BF16)
    for k in range(parts.shape[0] // group):
        out[k * group : (k + 1) * group, :] = whole


def total_parts(parts, share):
    return pl.pallas_call(
        total_kernel,
        out_shape=jax.ShapeDtypeStruct(parts.shape, BF16),
        in_specs=[VMEM],
        out_specs=VMEM,
        scratch_shapes=[pltpu.VMEM((TILE * share, 128), F32)],
        compiler_params=pltpu.CompilerParams(vmem_limit_bytes=8 * 1024 * 1024),
        cost_estimate=cost(3),
        name="total_parts",
    )(parts)


def unpack_kernel(packed_ref, *out_refs):
    flat_ref = packed_ref
    row = 0
    for out_ref in out_refs:
        depth, columns = out_ref.shape
        for k in range(columns // 128):
            out_ref[:, k * 128 : (k + 1) * 128] = flat_ref[row : row + depth, :].astype(F32)
            row += depth


def unpack(flat, shapes):
    return pl.pallas_call(
        unpack_kernel,
        out_shape=tuple(jax.ShapeDtypeStruct(shape, F32) for shape in shapes),
        in_specs=[VMEM],
        out_specs=tuple(VMEM for _ in shapes),
        compiler_params=pltpu.CompilerParams(vmem_limit_bytes=12 * 1024 * 1024),
        cost_estimate=cost(3),
        name="unpack_grads",
    )(flat)


BOTH = ("node", "rep")


def exchange(rows):
    pairs = lax.optimization_barrier(rows.reshape(rows.shape[0] // 2, 2, 128))
    pairs = lax.all_to_all(pairs, BOTH, split_axis=0, concat_axis=0, tiled=True)
    return lax.optimization_barrier(pairs).reshape(rows.shape)


def local(
    memory, req_rows, src_slot, dst_slot, nbr_slot, event_time, nbr_time, frequency, emb_grad,
    w_input, w_hidden, w_time, w_query, w_key, w_value, w_out,
):
    weights = (w_input, w_hidden, w_time, w_query, w_key, w_value, w_out)
    requests = req_rows[0]
    owners, capacity = requests.shape
    width = memory.shape[1]
    reps = lax.axis_size("rep")
    half = capacity // 2
    words = lax.optimization_barrier(paired(requests[:, :half], requests[:, half:]).reshape(owners, 1, half))
    asked = lax.all_to_all(words, "node", split_axis=0, concat_axis=0, tiled=True)
    asked = asked.reshape(owners, half)
    served = serve(asked.reshape(-1), memory).reshape(owners, capacity, width)
    fetched = lax.all_to_all(served, "node", split_axis=0, concat_axis=0, tiled=True)
    fetched = fetched.reshape(owners * capacity, width)
    lead = asked[:, :UCAP] & 0xFFFF
    turned = [lead] + [
        lax.ppermute(lead, "rep", [(i, (i + k) % reps) for i in range(reps)]) for k in range(1, reps)
    ]
    touched = jnp.stack(turned).reshape(-1)
    place = lax.axis_index("rep").astype(jnp.int32).reshape(1)
    events, nbrs = nbr_slot.shape
    nbr_index = (2 * nbr_slot).reshape(events // GROUP, GROUP, nbrs).transpose(0, 2, 1).reshape(-1)
    spacing = (event_time[:, None] - nbr_time).astype(F32)
    spacing = spacing.reshape(events // GROUP, GROUP, nbrs).transpose(0, 2, 1).reshape(1, -1)
    phase, timed = phase_step(spacing, frequency, w_time)
    fetched, touched, nbr_index, phase, timed = lax.optimization_barrier(
        (fetched, touched, nbr_index, phase, timed)
    )
    mem_src, mem_dst, change = memory_step(src_slot, dst_slot, fetched, w_input, w_hidden, reps)
    updates = lax.all_to_all(change.reshape(owners * reps * UCAP, width), BOTH, split_axis=0, concat_axis=0, tiled=True)
    shapes = (w_input.shape, w_hidden.shape, w_time.shape, w_query.shape, w_key.shape, w_value.shape, w_out.shape)
    used = sum(shape[0] * shape[1] for shape in shapes) // 128
    devices = owners * reps
    share = used // devices
    grads = events_step(nbr_index, fetched, phase, timed, mem_src, mem_dst, emb_grad, weights, devices * share)
    grads, updates = lax.optimization_barrier((grads, updates))
    parts = exchange(grads)
    summed = total_parts(parts, share)
    flat = exchange(summed)
    new_memory = merge(place, touched, updates, memory)
    return (new_memory, *unpack(flat, shapes))


def solution(mesh):
    split = P(BOTH)
    placed = (
        P("node", None), P(BOTH, None, None), split, split, P(BOTH, None), split, P(BOTH, None),
        P(), P(BOTH, None), P(), P(), P(), P(), P(), P(), P(),
    )
    return jax.shard_map(
        local,
        mesh=mesh,
        in_specs=placed,
        out_specs=(P("node", None), P(), P(), P(), P(), P(), P(), P()),
        check_vma=False,
    )
```
